256 devices in a mesh: stn: 32 (over y, z), tm: 8 (over x, core).
Axes of the slice: x: 4, y: 4, z: 8, core: 2. Of those that a mesh axis runs over, the one named last changes fastest.
Arguments:
- voltages: bfloat16 [2, 512, 32, 16384], P(None, 'stn', None, 'tm'), may hold values from -6 to 6
- fir_taps: float32 [16, 64], replicated, may hold values from -1.5 to 1.5
Outputs:
- visibilities: bfloat16 [32, 64, 2, 512, 512], P('stn', 'tm')
The draws below stay inside these ranges and needn't reach their ends.
All inputs are finite; a program needn't handle non-finite values.
Results may differ from the reference program's by a relative error of at most 0.0052.
Values may be sent and summed in bfloat16 or wider, within the bound.
A program may use at most 128 MiB of HBM per device.

```python
import math
import jax
import jax.numpy as jnp
from jax import lax

NINP = 512
CH = 64
TAPS = 16
SUBBANDS = 32
SAMPLES = 16384
NSPEC = 256


def steps_of(rng, shape, shards, low, top_value):
    factor_of = 1.0
    for axis_at, parts in shards:
        heights = jax.random.uniform(jax.random.fold_in(jax.random.fold_in(rng, 6), axis_at), (parts,), jnp.float32, low / len(shards), top_value / len(shards))
        factor_of = factor_of * jnp.repeat(jnp.exp(heights), shape[axis_at] // parts).reshape((-1,) + (1,) * (len(shape) - 1 - axis_at))
    return factor_of


def bell_draw(rng, dims, spread, most, pieces=(), kind=jnp.bfloat16):
    loudness = steps_of(rng, dims, pieces, -0.22, 0.18) if pieces else 1.0
    drawn = jax.random.normal(rng, dims, jnp.float32) * spread * loudness
    return jnp.minimum(jnp.maximum(drawn, -most), most).astype(kind)


def setup_inputs(seed: int = 0) -> dict:
    key_list = jax.random.split(jax.random.key(seed), 3)
    voltages = bell_draw(key_list[0], (2, NINP, SUBBANDS, SAMPLES), 1.0, 6.0, ((1, 32), (3, 8)))
    fir_taps = bell_draw(key_list[1], (TAPS, CH), TAPS ** -0.5, 1.5, (), jnp.float32)
    return {"voltages": voltages, "fir_taps": fir_taps}


def dft_tables(count):
    index = jnp.arange(count, dtype=jnp.int32)
    product = index[:, None] * index[None, :] % count
    angle = product.astype(jnp.float32) * (2.0 * math.pi / count)
    return (jnp.cos(angle), jnp.sin(angle))

def make_spectra(extended, fir_taps, spec_count):
    taps, branches = fir_taps.shape
    frames = extended.reshape(extended.shape[:-1] + (spec_count + taps - 1, branches)).astype(jnp.float32)
    filtered = jnp.zeros(frames.shape[:-2] + (spec_count, branches), jnp.float32)
    for tap_index in range(taps):
        begin = taps - 1 - tap_index
        filtered = filtered + fir_taps[tap_index] * frames[..., begin:begin + spec_count, :]
    cosine, sine_table = dft_tables(branches)
    high = lax.Precision.HIGHEST
    scale = 1.0 / math.sqrt(branches)
    real_in = filtered[0]
    imag_in = filtered[1]
    real_out = (jnp.einsum('...b,bk->...k', real_in, cosine, precision=high) + jnp.einsum('...b,bk->...k', imag_in, sine_table, precision=high)) * scale
    imag_out = (jnp.einsum('...b,bk->...k', imag_in, cosine, precision=high) - jnp.einsum('...b,bk->...k', real_in, sine_table, precision=high)) * scale
    return (real_out.astype(jnp.bfloat16), imag_out.astype(jnp.bfloat16))

def reference(voltages, fir_taps):
    history_len = (TAPS - 1) * CH

    def one_subband(samples):
        extended = jnp.concatenate([jnp.zeros((2, NINP, history_len), jnp.bfloat16), samples], axis=2)
        real_part, imag_part = make_spectra(extended, fir_taps, NSPEC)

        def one_channel(channel):
            stacked = jnp.concatenate([real_part[:, :, channel], imag_part[:, :, channel]], axis=0)
            gram = jnp.dot(stacked, stacked.T, preferred_element_type=jnp.float32)
            vis_real = gram[:NINP, :NINP] + gram[NINP:, NINP:]
            vis_imag = gram[NINP:, :NINP] - gram[:NINP, NINP:]
            return (jnp.stack([vis_real, vis_imag], 0) * (1.0 / NSPEC)).astype(jnp.bfloat16)
        return lax.map(one_channel, jnp.arange(CH, dtype=jnp.int32))
    return lax.map(one_subband, jnp.moveaxis(voltages, 2, 0))
```

```python
import functools
import math

import jax
import jax.numpy as jnp
import numpy as np
from jax import lax
from jax.experimental import pallas as pl
from jax.experimental.pallas import tpu as pltpu
from jax.sharding import PartitionSpec as P

MESH = pl.DeviceIdType.MESH
F32 = jnp.float32
BF16 = jnp.bfloat16

NY, NZ, NT = 4, 8, 8
STEPS = 8
ROWS = 16
LANES = NZ * ROWS
N = 2048
HIST = 1024
WIN = 1536
CH = 64
COS_ROWS = 34 * 8
SIN_ROWS = 32 * 8
AHEAD = 2
RELAY_1 = 6
NT_DIMS = (((1,), (1,)), ((), ()))


def trig_rows():
    b = np.arange(128) % CH
    rows = []
    for k in range(34):
        rows.append(np.cos(2 * np.pi * ((k * b) % CH) / CH))
    for k in range(32):
        rows.append(np.sin(2 * np.pi * ((k * b) % CH) / CH))
    table = np.stack(rows) / math.sqrt(CH)
    return np.repeat(table, 8, axis=0).astype(np.float32)


def comm_kernel(
    v_ref, taps_ref, trig_ref, out_ref,
    vbuf, sb, recv, jx, spec, w_hi, w_lo, ppad, t16, rc, rs, relay,
    v_sem, zs, zr, fr, rr, hs, hr, xs, xr, xl,
):
    stn = lax.axis_index("stn")
    tm = lax.axis_index("tm")
    y = lax.div(stn, NZ)
    z = lax.rem(stn, NZ)

    barrier = pltpu.get_barrier_semaphore()

    def greet_stn(i, _):
        pl.semaphore_signal(
            barrier, inc=1, device_id=(lax.rem(stn + i, NY * NZ), tm), device_id_type=MESH
        )
        return 0

    def greet_tm(i, _):
        pl.semaphore_signal(
            barrier, inc=1, device_id=(stn, lax.rem(tm + i, NT)), device_id_type=MESH
        )
        return 0

    def v_copy(i):
        qt, h = i // 2, i % 2
        return pltpu.make_async_copy(
            v_ref.at[:, pl.ds(h * 8, 8), pl.ds(qt * 16, 16), :], vbuf.at[i], v_sem.at[i]
        )

    for i in range(4):
        v_copy(i).start()
    lax.fori_loop(1, NY * NZ, greet_stn, 0)
    lax.fori_loop(1, NT, greet_tm, 0)

    def relayout(j):
        d, h = lax.div(j, 2), lax.rem(j, 2)
        yt = lax.rem(y + d, NY)
        at = lax.div(yt, 2) * 2 + h
        odd = lax.rem(yt, 2)
        o = lax.broadcasted_iota(jnp.int32, (LANES, 256), 0)
        c = lax.broadcasted_iota(jnp.int32, (LANES, 256), 1)
        want = ((o >> 3) & 1) * 128 + (o & 7) * 16 + odd * 8 + (o >> 4)
        perm = jnp.where(c == want, 1.0, 0.0).astype(BF16)
        for lane in range(0, N, 512):
            x = vbuf[at, :, :, :, lane : lane + 512].reshape(256, 512)
            turned = jnp.dot(perm, x, preferred_element_type=F32).astype(BF16)
            sb[j, :, :, lane : lane + 512] = turned.reshape(NZ, ROWS, 512)

    def z_copy(j, dz, first=0, count=N, sems=None):
        zt = lax.rem(z + dz, NZ)
        yt = lax.rem(y + lax.div(j, 2), NY)
        return pltpu.make_async_remote_copy(
            src_ref=sb.at[j, zt, :, pl.ds(first, count)],
            dst_ref=recv.at[j, z, :, pl.ds(HIST + first, count)],
            send_sem=zs.at[j],
            recv_sem=zr.at[j],
            device_id=(yt * NZ + zt, tm),
            device_id_type=MESH,
        )

    def own_copy(j):
        return pltpu.make_async_copy(
            sb.at[j, z], recv.at[j, z, :, pl.ds(HIST, N)], zr.at[j]
        )

    def relay_copy(j):
        zt = lax.rem(z + 4, NZ)
        return pltpu.make_async_remote_copy(
            src_ref=sb.at[j, zt, :, pl.ds(1024, 1024)],
            dst_ref=relay.at[j],
            send_sem=zs.at[j],
            recv_sem=rr.at[j],
            device_id=(y * NZ + lax.rem(z + RELAY_1, NZ), tm),
            device_id_type=MESH,
        )

    def forward_copy(j):
        source = lax.rem(z + NZ - RELAY_1, NZ)
        yt = lax.rem(y + lax.div(j, 2), NY)
        return pltpu.make_async_remote_copy(
            src_ref=relay.at[j],
            dst_ref=recv.at[j, source, :, pl.ds(HIST + 1024, 1024)],
            send_sem=fr.at[j],
            recv_sem=zr.at[j],
            device_id=(yt * NZ + lax.rem(z + 12 - RELAY_1, NZ), tm),
            device_id_type=MESH,
        )

    def send_step(j):
        relayout(j)
        if RELAY_1:
            relay_copy(j).start()
            z_copy(j, 4, 0, 1024).start()
        else:
            z_copy(j, 4).start()
        for dz in (3, 5, 2, 6, 1, 7):
            z_copy(j, dz).start()

        @pl.when(j < 2)
        def _():
            own_copy(j).start()

        @pl.when(j >= 2)
        def _():
            z_copy(j, 0).start()

    def forward(j):
        if RELAY_1:
            relay_copy(j).wait_recv()
            forward_copy(j).start()

    def wait_step(j):
        whole = recv.at[j, :, :, pl.ds(HIST, N)]
        pltpu.make_async_copy(whole, whole, zr.at[j]).wait()

    def halo_copy(j):
        return pltpu.make_async_remote_copy(
            src_ref=recv.at[j, :, :, pl.ds(N, HIST)],
            dst_ref=recv.at[j, :, :, pl.ds(0, HIST)],
            send_sem=hs.at[j],
            recv_sem=hr.at[j],
            device_id=(stn, lax.rem(tm + 1, NT)),
            device_id_type=MESH,
        )

    def slot_of(j):
        return lax.rem(y + NY - lax.div(j, 2), NY) * 2 + lax.rem(j, 2)

    def x_copy(j, gp, o):
        to = lax.rem(tm + o, NT)
        return pltpu.make_async_remote_copy(
            src_ref=spec.at[j, gp, pl.ds(to * 8, 8)],
            dst_ref=out_ref.at[tm, slot_of(j), gp],
            send_sem=xs.at[j],
            recv_sem=xr.at[j],
            device_id=(stn, to),
            device_id_type=MESH,
        )

    def x_own(j, gp):
        return pltpu.make_async_copy(
            spec.at[j, gp, pl.ds(tm * 8, 8)], out_ref.at[tm, slot_of(j), gp], xl.at[j]
        )

    def turn_complex(j, lane):
        o = lax.broadcasted_iota(jnp.int32, (LANES, LANES), 0)
        c = lax.broadcasted_iota(jnp.int32, (LANES, LANES), 1)
        im = (o >> 3) & 1
        sign = (1 - 2 * im).astype(F32)
        turn = jnp.where(c == o + 8 - 16 * im, sign, 0.0).astype(BF16)
        x = recv[j, :, :, lane : lane + 512].reshape(LANES, 512)
        jx[:, lane : lane + 512] = jnp.dot(turn, x, preferred_element_type=F32).astype(BF16)

    def spectra(j, gp):
        lo0 = 1024 * gp
        lo1 = lo0 + 512

        def both(w0, w1, x):
            hi = lax.dot_general(w_hi[w0:w1, :], x, NT_DIMS, preferred_element_type=F32)
            lo = lax.dot_general(w_lo[w0:w1, :], x, NT_DIMS, preferred_element_type=F32)
            return hi + lo

        x = jnp.concatenate(
            [
                recv[j, :, :, lo0 : lo0 + WIN].reshape(LANES, WIN),
                recv[j, :, :, lo1 : lo1 + WIN].reshape(LANES, WIN),
            ],
            axis=0,
        )
        rc[...] = both(0, COS_ROWS, x)
        x = jnp.concatenate([jx[:, lo0 : lo0 + WIN], jx[:, lo1 : lo1 + WIN]], axis=0)
        rs[...] = both(COS_ROWS, COS_ROWS + SIN_ROWS, x)

        def put(k, a):
            tile = jnp.concatenate([a[:, :128], a[:, 128:]], axis=0)
            spec[j, gp, k] = tile.astype(BF16)

        put(0, rc[0:8, :])
        put(32, rc[256:264, :])
        for k in range(1, 32):
            c = rc[8 * k : 8 * k + 8, :]
            s = rs[8 * k : 8 * k + 8, :]
            put(k, c + s)
            put(64 - k, c - s)

    def send_spectra(j, gp):
        x_own(j, gp).start()

        def start(o, _):
            x_copy(j, gp, o).start()
            return 0

        lax.fori_loop(1, NT, start, 0)

    for i in range(4):
        v_copy(i).wait()
    relayout(0)
    pl.semaphore_wait(barrier, NY * NZ - 1 + NT - 1)

    def prime(j, _):
        send_step(j)
        return 0

    lax.fori_loop(0, AHEAD, prime, 0)

    half = lax.broadcasted_iota(jnp.int32, (16, 128), 1) < CH
    taps = jnp.concatenate([taps_ref[...], taps_ref[...]], axis=1)
    ppad[...] = jnp.zeros_like(ppad)
    ppad[8:24, :] = jnp.where(half, taps, 0.0)
    ppad[9:25, :] = ppad[9:25, :] + jnp.where(half, 0.0, taps)
    for i in range(WIN // 128):
        tile = ppad[24 - 2 * i : 32 - 2 * i, :]
        t16[:, 128 * i : 128 * i + 128] = jnp.concatenate([tile, tile], axis=0)

    def weights(i, _):
        rows = pl.ds(pl.multiple_of(i * 16, 16), 16)
        trig = trig_ref[rows, :]
        for t in range(WIN // 128):
            lanes = slice(128 * t, 128 * t + 128)
            w = t16[:, lanes] * trig
            hi = w.astype(BF16)
            w_hi[rows, lanes] = hi
            w_lo[rows, lanes] = (w - hi.astype(F32)).astype(BF16)
        return 0

    lax.fori_loop(0, (COS_ROWS + SIN_ROWS) // 16, weights, 0)

    forward(0)

    def step(j, _):
        @pl.when(j + AHEAD < STEPS)
        def _():
            send_step(j + AHEAD)

        wait_step(j)

        @pl.when(tm < NT - 1)
        def _():
            halo_copy(j).start()

        for lane in range(HIST, HIST + N, 512):
            turn_complex(j, lane)
        spectra(j, 1)
        send_spectra(j, 1)

        @pl.when(j + 1 < STEPS)
        def _():
            forward(j + 1)

        @pl.when(tm > 0)
        def _():
            halo_copy(j).wait_recv()

        @pl.when(tm == 0)
        def _():
            recv[j, :, :, 0:HIST] = jnp.zeros((NZ, ROWS, HIST), BF16)

        for lane in range(0, HIST, 512):
            turn_complex(j, lane)
        spectra(j, 0)
        send_spectra(j, 0)
        return 0

    lax.fori_loop(0, STEPS, step, 0)

    def finish(j, _):
        @pl.when(j < 2)
        def _():
            part = sb.at[j, pl.ds(0, NZ - 1)]
            pltpu.make_async_copy(part, part, zs.at[j]).wait()

        @pl.when(j >= 2)
        def _():
            part = sb.at[j]
            pltpu.make_async_copy(part, part, zs.at[j]).wait()

        if RELAY_1:
            forward_copy(j).wait_send()

        @pl.when(tm < NT - 1)
        def _():
            halo_copy(j).wait_send()

        mine = spec.at[j, :, pl.ds(0, 8)]
        pltpu.make_async_copy(mine, mine, xl.at[j]).wait()
        others = spec.at[j, :, pl.ds(0, 56)]
        pltpu.make_async_copy(others, others, xs.at[j]).wait()
        pltpu.make_async_copy(others, others, xr.at[j]).wait()
        return 0

    lax.fori_loop(0, STEPS, finish, 0)


def gram_kernel(x_ref, order_ref, out_ref):
    def inputs(yy):
        a = jnp.concatenate(
            [
                x_ref[:, 2 * yy, :, 0].reshape(256, 128),
                x_ref[:, 2 * yy + 1, :, 0].reshape(256, 128),
            ],
            axis=1,
        )
        return lax.dot_general(
            order_ref[...], a, NT_DIMS, preferred_element_type=F32
        ).astype(BF16)

    parts = [inputs(yy) for yy in range(NY)]
    re = jnp.concatenate([t[:128] for t in parts], axis=0)
    im = jnp.concatenate([t[128:] for t in parts], axis=0)
    u = jnp.concatenate([re, im], axis=1)
    w = jnp.concatenate([im, -re], axis=1)
    scale = 1.0 / 256
    real = lax.dot_general(u, u, NT_DIMS, preferred_element_type=F32)
    out_ref[0, 0, 0] = (real * scale).astype(BF16)
    imag = lax.dot_general(w, u, NT_DIMS, preferred_element_type=F32)
    out_ref[0, 0, 1] = (imag * scale).astype(BF16)


def input_order():
    m = np.zeros((256, 256), np.float32)
    for ri in range(2):
        for zz in range(8):
            for h in range(2):
                for r in range(8):
                    m[ri * 128 + zz * 16 + h * 8 + r, h * 128 + zz * 16 + ri * 8 + r] = 1.0
    return m


def body(voltages, fir_taps):
    dma = pltpu.SemaphoreType.DMA
    any_space = pl.BlockSpec(memory_space=pl.ANY)
    in_vmem = pl.BlockSpec(memory_space=pltpu.VMEM)
    gathered = pl.pallas_call(
        comm_kernel,
        out_shape=jax.ShapeDtypeStruct((NT, STEPS, 2, 8, 16, 128), BF16),
        in_specs=[any_space, in_vmem, in_vmem],
        out_specs=any_space,
        scratch_shapes=[
            pltpu.VMEM((4, 2, 8, 16, N), BF16),
            pltpu.VMEM((STEPS, NZ, ROWS, N), BF16),
            pltpu.VMEM((STEPS, NZ, ROWS, HIST + N), BF16),
            pltpu.VMEM((LANES, HIST + N), BF16),
            pltpu.VMEM((STEPS, 2, CH, 16, 128), BF16),
            pltpu.VMEM((COS_ROWS + SIN_ROWS, WIN), BF16),
            pltpu.VMEM((COS_ROWS + SIN_ROWS, WIN), BF16),
            pltpu.VMEM((32, 128), F32),
            pltpu.VMEM((16, WIN), F32),
            pltpu.VMEM((COS_ROWS, 256), F32),
            pltpu.VMEM((SIN_ROWS, 256), F32),
            pltpu.VMEM((STEPS, ROWS, 1024), BF16),
            dma((4,)),
        ]
        + [dma((STEPS,))] * 9,
        compiler_params=pltpu.CompilerParams(
            collective_id=0, has_side_effects=True, vmem_limit_bytes=48 * 2**20
        ),
        name="exchange",
    )(voltages, fir_taps, jnp.asarray(trig_rows()))
    return pl.pallas_call(
        gram_kernel,
        grid=(8,),
        out_shape=jax.ShapeDtypeStruct((1, 8, 2, 512, 512), BF16),
        in_specs=[
            pl.BlockSpec((NT, STEPS, 2, 1, 16, 128), lambda k: (0, 0, 0, k, 0, 0)),
            pl.BlockSpec((256, 256), lambda k: (0, 0)),
        ],
        out_specs=pl.BlockSpec((1, 1, 2, 512, 512), lambda k: (0, k, 0, 0, 0)),
        compiler_params=pltpu.CompilerParams(vmem_limit_bytes=32 * 2**20),
        name="gram",
    )(gathered, jnp.asarray(input_order(), BF16))


def solution(mesh):
    return jax.shard_map(
        body,
        mesh=mesh,
        in_specs=(P(None, "stn", None, "tm"), P()),
        out_specs=P("stn", "tm", None, None, None),
        check_vma=False,
    )
```

```python
import functools
import math

import jax
import jax.numpy as jnp
import numpy as np
from jax import lax
from jax.experimental import pallas as pl
from jax.experimental.pallas import tpu as pltpu
from jax.sharding import PartitionSpec as P

MESH = pl.DeviceIdType.MESH
F32 = jnp.float32
BF16 = jnp.bfloat16

NY, NZ, NT = 4, 8, 8
STEPS = 8
ROWS = 16
LANES = NZ * ROWS
N = 2048
HIST = 1024
WIN = 1536
CH = 64
COS_ROWS = 34 * 8
SIN_ROWS = 32 * 8
AHEAD = 2
FIRST = 6
ORDER = (1, 7, 2, 6, 3, 5, 4, 0)
NT_DIMS = (((1,), (1,)), ((), ()))


def trig_rows():
    b = np.arange(128) % CH
    rows = []
    for k in range(34):
        rows.append(np.cos(2 * np.pi * ((k * b) % CH) / CH))
    for k in range(32):
        rows.append(np.sin(2 * np.pi * ((k * b) % CH) / CH))
    table = np.stack(rows) / math.sqrt(CH)
    return np.repeat(table, 8, axis=0).astype(np.float32)


def comm_kernel(
    v_ref, taps_hbm, trig_hbm, u_ref,
    vbuf, taps_ref, trig_ref, sb, recv, jx, spec, xg, ub, zbuf,
    w_hi, w_lo, ppad, t16, rc, rs,
    v_sem, c_sem, zs, zr, hs, hr, xs, xr, us,
):
    stn = lax.axis_index("stn")
    tm = lax.axis_index("tm")
    y = lax.div(stn, NZ)
    z = lax.rem(stn, NZ)

    barrier = pltpu.get_barrier_semaphore()

    def greet_stn(i, _):
        pl.semaphore_signal(
            barrier, inc=1, device_id=(lax.rem(stn + i, NY * NZ), tm), device_id_type=MESH
        )
        return 0

    def greet_tm(i, _):
        pl.semaphore_signal(
            barrier, inc=1, device_id=(stn, lax.rem(tm + i, NT)), device_id_type=MESH
        )
        return 0

    def v_copy(i):
        qt, h = i // 2, i % 2
        return pltpu.make_async_copy(
            v_ref.at[:, pl.ds(h * 8, 8), pl.ds(qt * 16, 16), :], vbuf.at[i], v_sem.at[i]
        )

    taps_copy = pltpu.make_async_copy(taps_hbm, taps_ref, c_sem.at[0])
    trig_copy = pltpu.make_async_copy(trig_hbm, trig_ref, c_sem.at[1])
    for i in range(4):
        v_copy(i).start()
    taps_copy.start()
    trig_copy.start()
    lax.fori_loop(1, NY * NZ, greet_stn, 0)
    lax.fori_loop(1, NT, greet_tm, 0)

    def relayout(j, put):
        d, h = lax.div(j, 2), lax.rem(j, 2)
        yt = lax.rem(y + d, NY)
        at = lax.div(yt, 2) * 2 + h
        odd = lax.rem(yt, 2)
        o = lax.broadcasted_iota(jnp.int32, (LANES, 256), 0)
        c = lax.broadcasted_iota(jnp.int32, (LANES, 256), 1)
        want = ((o >> 3) & 1) * 128 + (o & 7) * 16 + odd * 8 + (o >> 4)
        perm = jnp.where(c == want, 1.0, 0.0).astype(BF16)
        for lane in range(0, N, 512):
            x = vbuf[at, :, :, :, lane : lane + 512].reshape(256, 512)
            turned = jnp.dot(perm, x, preferred_element_type=F32).astype(BF16)
            put(lane, turned.reshape(NZ, ROWS, 512))

    def z_target(j, dz):
        zt = lax.rem(z + dz, NZ)
        yt = lax.rem(y + lax.div(j, 2), NY)
        return zt, (yt * NZ + zt, tm)

    def z_copy(j, dz):
        zt, to = z_target(j, dz)
        return pltpu.make_async_remote_copy(
            src_ref=sb.at[j, zt],
            dst_ref=recv.at[j, z, :, pl.ds(HIST, N)],
            send_sem=zs.at[j],
            recv_sem=zr.at[j],
            device_id=to,
            device_id_type=MESH,
        )

    def own_copy(j):
        return pltpu.make_async_copy(
            sb.at[j, z], recv.at[j, z, :, pl.ds(HIST, N)], zr.at[j]
        )

    def late_copy(j, dz):
        zt, to = z_target(j, dz)
        ri = lax.rem(j, 2)
        at = pl.multiple_of(y * 128 + z * 16, 16)
        return pltpu.make_async_remote_copy(
            src_ref=zbuf.at[zt, ri],
            dst_ref=u_ref.at[ri, pl.ds(at, 16), :],
            send_sem=zs.at[j],
            recv_sem=zr.at[j],
            device_id=to,
            device_id_type=MESH,
        )

    def send_step(j):
        def put(lane, tile):
            sb[j, :, :, lane : lane + 512] = tile

        relayout(j, put)
        for dz in ORDER[:-1]:
            z_copy(j, dz).start()

        @pl.when(j < 2)
        def _():
            own_copy(j).start()

        @pl.when(j >= 2)
        def _():
            z_copy(j, 0).start()

    def send_late(j):
        for dz in ORDER:
            late_copy(j, dz).start()

    def wait_step(j):
        whole = recv.at[j, :, :, pl.ds(HIST, N)]
        pltpu.make_async_copy(whole, whole, zr.at[j]).wait()

    def halo_copy(j):
        return pltpu.make_async_remote_copy(
            src_ref=recv.at[j, :, :, pl.ds(N, HIST)],
            dst_ref=recv.at[j, :, :, pl.ds(0, HIST)],
            send_sem=hs.at[j],
            recv_sem=hr.at[j],
            device_id=(stn, lax.rem(tm + 1, NT)),
            device_id_type=MESH,
        )

    def send_halo(j):
        @pl.when(tm < NT - 1)
        def _():
            halo_copy(j).start()

    def wait_halo(j):
        @pl.when(tm > 0)
        def _():
            halo_copy(j).wait_recv()

        @pl.when(tm == 0)
        def _():
            recv[j, :, :, 0:HIST] = jnp.zeros((NZ, ROWS, HIST), BF16)

    def x_copy(j, gp, o):
        to = lax.rem(tm + o, NT)
        return pltpu.make_async_remote_copy(
            src_ref=spec.at[j, gp, pl.ds(to * 8, 8)],
            dst_ref=xg.at[j, tm, gp],
            send_sem=xs.at[j],
            recv_sem=xr.at[j],
            device_id=(stn, to),
            device_id_type=MESH,
        )

    def x_own(j, gp):
        return pltpu.make_async_copy(
            spec.at[j, gp, pl.ds(tm * 8, 8)], xg.at[j, tm, gp], xr.at[j]
        )

    def turn_complex(j, lane):
        o = lax.broadcasted_iota(jnp.int32, (LANES, LANES), 0)
        c = lax.broadcasted_iota(jnp.int32, (LANES, LANES), 1)
        im = (o >> 3) & 1
        sign = (1 - 2 * im).astype(F32)
        turn = jnp.where(c == o + 8 - 16 * im, sign, 0.0).astype(BF16)
        x = recv[j, :, :, lane : lane + 512].reshape(LANES, 512)
        jx[:, lane : lane + 512] = jnp.dot(turn, x, preferred_element_type=F32).astype(BF16)

    def spectra(j, gp):
        lo0 = 1024 * gp
        lo1 = lo0 + 512

        def both(w0, w1, x):
            hi = lax.dot_general(w_hi[w0:w1, :], x, NT_DIMS, preferred_element_type=F32)
            lo = lax.dot_general(w_lo[w0:w1, :], x, NT_DIMS, preferred_element_type=F32)
            return hi + lo

        x = jnp.concatenate(
            [
                recv[j, :, :, lo0 : lo0 + WIN].reshape(LANES, WIN),
                recv[j, :, :, lo1 : lo1 + WIN].reshape(LANES, WIN),
            ],
            axis=0,
        )
        rc[...] = both(0, COS_ROWS, x)
        x = jnp.concatenate([jx[:, lo0 : lo0 + WIN], jx[:, lo1 : lo1 + WIN]], axis=0)
        rs[...] = both(COS_ROWS, COS_ROWS + SIN_ROWS, x)

        def put(k, a):
            tile = jnp.concatenate([a[:, :128], a[:, 128:]], axis=0)
            spec[j, gp, k] = tile.astype(BF16)

        put(0, rc[0:8, :])
        put(32, rc[256:264, :])
        for k in range(1, 32):
            c = rc[8 * k : 8 * k + 8, :]
            s = rs[8 * k : 8 * k + 8, :]
            put(k, c + s)
            put(64 - k, c - s)

    def send_spectra(j, gp):
        def start(o, _):
            x_copy(j, gp, o).start()
            return 0

        lax.fori_loop(1, NT, start, 0)
        x_own(j, gp).start()

    def filterbank(j):
        for lane in range(HIST, HIST + N, 512):
            turn_complex(j, lane)
        spectra(j, 1)
        send_spectra(j, 1)
        wait_halo(j)
        for lane in range(0, HIST, 512):
            turn_complex(j, lane)
        spectra(j, 0)
        send_spectra(j, 0)

    def wait_spectra(j):
        pltpu.make_async_copy(spec.at[j], spec.at[j], xr.at[j]).wait()

    def turn_pair(d, want, put):
        wait_spectra(2 * d)
        wait_spectra(2 * d + 1)
        c = lax.broadcasted_iota(jnp.int32, (256, 256), 1)
        perm = jnp.where(c == want, 1.0, 0.0).astype(BF16)

        def channel(k, _):
            a = jnp.concatenate(
                [
                    xg[2 * d, :, :, k].reshape(256, LANES),
                    xg[2 * d + 1, :, :, k].reshape(256, LANES),
                ],
                axis=1,
            )
            t = lax.dot_general(perm, a, NT_DIMS, preferred_element_type=F32)
            put(pl.ds(pl.multiple_of(k * 256, 256), 256), t.astype(BF16))
            return 0

        lax.fori_loop(0, 8, channel, 0)

    def u_copy(d):
        at = pl.multiple_of(lax.rem(y + NY - d, NY) * 128, 128)
        return pltpu.make_async_copy(ub.at[d], u_ref.at[:, pl.ds(at, 128), :], us.at[d])

    def turn_early(d):
        o = lax.broadcasted_iota(jnp.int32, (256, 256), 0)
        want = ((o >> 3) & 1) * 128 + ((o >> 4) & 7) * 16 + (o >> 7) * 8 + (o & 7)

        def put(lanes, t):
            ub[d, :, :, lanes] = t.reshape(2, 128, 256)

        turn_pair(d, want, put)
        u_copy(d).start()

    def turn_late():
        o = lax.broadcasted_iota(jnp.int32, (256, 256), 0)
        want = ((o >> 3) & 1) * 128 + (o >> 5) * 16 + ((o >> 4) & 1) * 8 + (o & 7)

        def put(lanes, t):
            zbuf[:, :, :, lanes] = t.reshape(NZ, 2, 16, 256)

        turn_pair(3, want, put)

    for i in range(4):
        v_copy(i).wait()
    pl.semaphore_wait(barrier, NY * NZ - 1 + NT - 1)

    def prime(j, _):
        send_step(j)
        return 0

    lax.fori_loop(0, AHEAD, prime, 0)

    def prime_late(j, _):
        def put(lane, tile):
            recv[j, :, :, HIST + lane : HIST + lane + 512] = tile

        relayout(j, put)
        send_halo(j)
        return 0

    lax.fori_loop(FIRST, STEPS, prime_late, 0)

    taps_copy.wait()
    trig_copy.wait()
    half = lax.broadcasted_iota(jnp.int32, (16, 128), 1) < CH
    taps = jnp.concatenate([taps_ref[...], taps_ref[...]], axis=1)
    ppad[...] = jnp.zeros_like(ppad)
    ppad[8:24, :] = jnp.where(half, taps, 0.0)
    ppad[9:25, :] = ppad[9:25, :] + jnp.where(half, 0.0, taps)
    for i in range(WIN // 128):
        tile = ppad[24 - 2 * i : 32 - 2 * i, :]
        t16[:, 128 * i : 128 * i + 128] = jnp.concatenate([tile, tile], axis=0)

    def weights(i, _):
        rows = pl.ds(pl.multiple_of(i * 16, 16), 16)
        trig = trig_ref[rows, :]
        for t in range(WIN // 128):
            lanes = slice(128 * t, 128 * t + 128)
            w = t16[:, lanes] * trig
            hi = w.astype(BF16)
            w_hi[rows, lanes] = hi
            w_lo[rows, lanes] = (w - hi.astype(F32)).astype(BF16)
        return 0

    lax.fori_loop(0, (COS_ROWS + SIN_ROWS) // 16, weights, 0)

    def step(i, _):
        j = jnp.where(i < 2, FIRST + i, i - 2)

        @pl.when(i >= 2)
        def _():
            @pl.when(j + AHEAD < FIRST)
            def _():
                send_step(j + AHEAD)

            @pl.when(j + AHEAD >= FIRST)
            def _():
                send_late(j + AHEAD)

            wait_step(j)
            send_halo(j)

        filterbank(j)

        @pl.when(j == LATE_AT)
        def _():
            turn_late()

        @pl.when((j == 3) | (j == 5))
        def _():
            turn_early(lax.div(j - 3, 2))

        return 0

    lax.fori_loop(0, STEPS, step, 0)
    turn_early(2)

    def finish(j, _):
        @pl.when(j < 2)
        def _():
            part = sb.at[j, pl.ds(0, NZ - 1)]
            pltpu.make_async_copy(part, part, zs.at[j]).wait()

        @pl.when(j >= 2)
        def _():
            part = sb.at[0]
            pltpu.make_async_copy(part, part, zs.at[j]).wait()

        @pl.when(j >= FIRST)
        def _():
            wait_step(j)

        @pl.when(tm < NT - 1)
        def _():
            halo_copy(j).wait_send()

        others = spec.at[j, :, pl.ds(0, 56)]
        pltpu.make_async_copy(others, others, xs.at[j]).wait()
        return 0

    lax.fori_loop(0, STEPS, finish, 0)
    for d in range(3):
        u_copy(d).wait()


LATE_AT = 1


def gram_kernel(u_ref, out_ref):
    re, im = u_ref[0], u_ref[1]
    u = jnp.concatenate([re, im], axis=1)
    w = jnp.concatenate([im, -re], axis=1)
    scale = 1.0 / 256
    real = lax.dot_general(u, u, NT_DIMS, preferred_element_type=F32)
    out_ref[0, 0, 0] = (real * scale).astype(BF16)
    imag = lax.dot_general(w, u, NT_DIMS, preferred_element_type=F32)
    out_ref[0, 0, 1] = (imag * scale).astype(BF16)


def body(voltages, fir_taps):
    dma = pltpu.SemaphoreType.DMA
    any_space = pl.BlockSpec(memory_space=pl.ANY)
    gathered = pl.pallas_call(
        comm_kernel,
        out_shape=jax.ShapeDtypeStruct((2, 512, 8 * 256), BF16),
        in_specs=[pl.BlockSpec(memory_space=pltpu.HBM)] * 3,
        out_specs=any_space,
        scratch_shapes=[
            pltpu.VMEM((4, 2, 8, 16, N), BF16),
            pltpu.VMEM((16, CH), F32),
            pltpu.VMEM((COS_ROWS + SIN_ROWS, 128), F32),
            pltpu.VMEM((FIRST, NZ, ROWS, N), BF16),
            pltpu.VMEM((STEPS, NZ, ROWS, HIST + N), BF16),
            pltpu.VMEM((LANES, HIST + N), BF16),
            pltpu.VMEM((STEPS, 2, CH, 16, 128), BF16),
            pltpu.VMEM((STEPS, NT, 2, 8, 16, 128), BF16),
            pltpu.VMEM((3, 2, 128, 8 * 256), BF16),
            pltpu.VMEM((NZ, 2, 16, 8 * 256), BF16),
            pltpu.VMEM((COS_ROWS + SIN_ROWS, WIN), BF16),
            pltpu.VMEM((COS_ROWS + SIN_ROWS, WIN), BF16),
            pltpu.VMEM((32, 128), F32),
            pltpu.VMEM((16, WIN), F32),
            pltpu.VMEM((COS_ROWS, 256), F32),
            pltpu.VMEM((SIN_ROWS, 256), F32),
            dma((4,)),
            dma((2,)),
        ]
        + [dma((STEPS,))] * 6
        + [dma((3,))],
        compiler_params=pltpu.CompilerParams(
            collective_id=0, has_side_effects=True, vmem_limit_bytes=48 * 2**20
        ),
        name="exchange",
    )(voltages, fir_taps, jnp.asarray(trig_rows()))
    return pl.pallas_call(
        gram_kernel,
        grid=(8,),
        out_shape=jax.ShapeDtypeStruct((1, 8, 2, 512, 512), BF16),
        in_specs=[pl.BlockSpec((2, 512, 256), lambda k: (0, 0, k))],
        out_specs=pl.BlockSpec((1, 1, 2, 512, 512), lambda k: (0, k, 0, 0, 0)),
        compiler_params=pltpu.CompilerParams(vmem_limit_bytes=16 * 2**20),
        name="gram",
    )(gathered)


def solution(mesh):
    return jax.shard_map(
        body,
        mesh=mesh,
        in_specs=(P(None, "stn", None, "tm"), P()),
        out_specs=P("stn", "tm", None, None, None),
        check_vma=False,
    )
```

```python
import functools
import math

import jax
import jax.numpy as jnp
from jax import lax
from jax.experimental import pallas as pl
from jax.experimental.pallas import tpu as pltpu
from jax.sharding import PartitionSpec as P

MESH = pl.DeviceIdType.MESH
F32 = jnp.float32
BF16 = jnp.bfloat16

NY, NZ, NT = 4, 8, 8
STEPS = 8
ROWS = 16
LANES = NZ * ROWS
N = 2048
HIST = 1024
WIN = 1536
CH = 64
COS_ROWS = 34 * 8
SIN_ROWS = 32 * 8
AHEAD = 2
FIRST = 6
ORDER = (1, 7, 2, 6, 3, 5, 4, 0)
NT_DIMS = (((1,), (1,)), ((), ()))


def comm_kernel(
    v_ref, taps_hbm, u_ref,
    vbuf, taps_ref, sb, recv, jx, spec, xg, ub, zbuf,
    w_hi, w_lo, ppad, t16, rc, rs,
    v_sem, c_sem, zs, zr, hs, hr, xs, xr, us,
):
    stn = lax.axis_index("stn")
    tm = lax.axis_index("tm")
    y = lax.div(stn, NZ)
    z = lax.rem(stn, NZ)

    barrier = pltpu.get_barrier_semaphore()

    def greet_stn(i, _):
        pl.semaphore_signal(
            barrier, inc=1, device_id=(lax.rem(stn + i, NY * NZ), tm), device_id_type=MESH
        )
        return 0

    def greet_tm(i, _):
        pl.semaphore_signal(
            barrier, inc=1, device_id=(stn, lax.rem(tm + i, NT)), device_id_type=MESH
        )
        return 0

    def v_copy(i):
        qt, h = lax.div(i, 2), lax.rem(i, 2)
        return pltpu.make_async_copy(
            v_ref.at[:, pl.ds(pl.multiple_of(h * 8, 8), 8), pl.ds(pl.multiple_of(qt * 16, 16), 16), :],
            vbuf.at[i],
            v_sem.at[i],
        )

    taps_copy = pltpu.make_async_copy(taps_hbm, taps_ref, c_sem.at[0])
    first = lax.div(y, 2) * 2
    pieces = (first, first + 1, 2 - first, 3 - first)
    for i in pieces:
        v_copy(i).start()
    taps_copy.start()
    lax.fori_loop(1, NY * NZ, greet_stn, 0)
    lax.fori_loop(1, NT, greet_tm, 0)

    def relayout(j, put):
        d, h = lax.div(j, 2), lax.rem(j, 2)
        yt = lax.rem(y + d, NY)
        at = lax.div(yt, 2) * 2 + h
        odd = lax.rem(yt, 2)
        o = lax.broadcasted_iota(jnp.int32, (LANES, 256), 0)
        c = lax.broadcasted_iota(jnp.int32, (LANES, 256), 1)
        want = ((o >> 3) & 1) * 128 + (o & 7) * 16 + odd * 8 + (o >> 4)
        perm = jnp.where(c == want, 1.0, 0.0).astype(BF16)
        for lane in range(0, N, 512):
            x = vbuf[at, :, :, :, lane : lane + 512].reshape(256, 512)
            turned = jnp.dot(perm, x, preferred_element_type=F32).astype(BF16)
            put(lane, turned.reshape(NZ, ROWS, 512))

    def z_target(j, dz):
        zt = lax.rem(z + dz, NZ)
        yt = lax.rem(y + lax.div(j, 2), NY)
        return zt, (yt * NZ + zt, tm)

    def z_copy(j, dz):
        zt, to = z_target(j, dz)
        return pltpu.make_async_remote_copy(
            src_ref=sb.at[j, zt],
            dst_ref=recv.at[j, z, :, pl.ds(HIST, N)],
            send_sem=zs.at[j],
            recv_sem=zr.at[j],
            device_id=to,
            device_id_type=MESH,
        )

    def own_copy(j):
        return pltpu.make_async_copy(
            sb.at[j, z], recv.at[j, z, :, pl.ds(HIST, N)], zr.at[j]
        )

    def late_copy(j, dz):
        zt, to = z_target(j, dz)
        ri = lax.rem(j, 2)
        at = pl.multiple_of(y * 128 + z * 16, 16)
        return pltpu.make_async_remote_copy(
            src_ref=zbuf.at[zt, ri],
            dst_ref=u_ref.at[ri, pl.ds(at, 16), :],
            send_sem=zs.at[j],
            recv_sem=zr.at[j],
            device_id=to,
            device_id_type=MESH,
        )

    def prepare(j):
        def put(lane, tile):
            sb[j, :, :, lane : lane + 512] = tile

        relayout(j, put)

    def send_step(j):
        for dz in ORDER[:-1]:
            z_copy(j, dz).start()

        @pl.when(j < 2)
        def _():
            own_copy(j).start()

        @pl.when(j >= 2)
        def _():
            z_copy(j, 0).start()

    def send_late(j):
        for dz in ORDER:
            late_copy(j, dz).start()

    def wait_step(j):
        whole = recv.at[j, :, :, pl.ds(HIST, N)]
        pltpu.make_async_copy(whole, whole, zr.at[j]).wait()

    def halo_copy(j):
        return pltpu.make_async_remote_copy(
            src_ref=recv.at[j, :, :, pl.ds(N, HIST)],
            dst_ref=recv.at[j, :, :, pl.ds(0, HIST)],
            send_sem=hs.at[j],
            recv_sem=hr.at[j],
            device_id=(stn, lax.rem(tm + 1, NT)),
            device_id_type=MESH,
        )

    def send_halo(j):
        @pl.when(tm < NT - 1)
        def _():
            halo_copy(j).start()

    def wait_halo(j):
        @pl.when(tm > 0)
        def _():
            halo_copy(j).wait_recv()

        @pl.when(tm == 0)
        def _():
            recv[j, :, :, 0:HIST] = jnp.zeros((NZ, ROWS, HIST), BF16)

    def x_copy(j, gp, o):
        to = lax.rem(tm + o, NT)
        return pltpu.make_async_remote_copy(
            src_ref=spec.at[j, gp, pl.ds(to * 8, 8)],
            dst_ref=xg.at[j, tm, gp],
            send_sem=xs.at[j],
            recv_sem=xr.at[j],
            device_id=(stn, to),
            device_id_type=MESH,
        )

    def x_own(j, gp):
        return pltpu.make_async_copy(
            spec.at[j, gp, pl.ds(tm * 8, 8)], xg.at[j, tm, gp], xr.at[j]
        )

    def turn_complex(j, lane):
        o = lax.broadcasted_iota(jnp.int32, (LANES, LANES), 0)
        c = lax.broadcasted_iota(jnp.int32, (LANES, LANES), 1)
        im = (o >> 3) & 1
        sign = (1 - 2 * im).astype(F32)
        turn = jnp.where(c == o + 8 - 16 * im, sign, 0.0).astype(BF16)
        x = recv[j, :, :, lane : lane + 512].reshape(LANES, 512)
        jx[:, lane : lane + 512] = jnp.dot(turn, x, preferred_element_type=F32).astype(BF16)

    def spectra(j, gp):
        lo0 = 1024 * gp
        lo1 = lo0 + 512

        def both(w0, w1, x):
            hi = lax.dot_general(w_hi[w0:w1, :], x, NT_DIMS, preferred_element_type=F32)
            lo = lax.dot_general(w_lo[w0:w1, :], x, NT_DIMS, preferred_element_type=F32)
            return hi + lo

        x = jnp.concatenate(
            [
                recv[j, :, :, lo0 : lo0 + WIN].reshape(LANES, WIN),
                recv[j, :, :, lo1 : lo1 + WIN].reshape(LANES, WIN),
            ],
            axis=0,
        )
        rc[...] = both(0, COS_ROWS, x)
        x = jnp.concatenate([jx[:, lo0 : lo0 + WIN], jx[:, lo1 : lo1 + WIN]], axis=0)
        rs[...] = both(COS_ROWS, COS_ROWS + SIN_ROWS, x)

        def put(k, a):
            tile = jnp.concatenate([a[:, :128], a[:, 128:]], axis=0)
            spec[j, gp, k] = tile.astype(BF16)

        put(0, rc[0:8, :])
        put(32, rc[256:264, :])
        for k in range(1, 32):
            c = rc[8 * k : 8 * k + 8, :]
            s = rs[8 * k : 8 * k + 8, :]
            put(k, c + s)
            put(64 - k, c - s)

    def send_spectra(j, gp):
        def start(o, _):
            x_copy(j, gp, o).start()
            return 0

        lax.fori_loop(1, NT, start, 0)
        x_own(j, gp).start()

    def filterbank(j):
        for lane in range(HIST, HIST + N, 512):
            turn_complex(j, lane)
        spectra(j, 1)
        send_spectra(j, 1)
        wait_halo(j)
        for lane in range(0, HIST, 512):
            turn_complex(j, lane)
        spectra(j, 0)
        send_spectra(j, 0)

    def wait_spectra(j):
        pltpu.make_async_copy(spec.at[j], spec.at[j], xr.at[j]).wait()

    def turn_pair(d, want, put):
        wait_spectra(2 * d)
        wait_spectra(2 * d + 1)
        c = lax.broadcasted_iota(jnp.int32, (256, 256), 1)
        perm = jnp.where(c == want, 1.0, 0.0).astype(BF16)

        def channel(k, _):
            a = jnp.concatenate(
                [
                    xg[2 * d, :, :, k].reshape(256, LANES),
                    xg[2 * d + 1, :, :, k].reshape(256, LANES),
                ],
                axis=1,
            )
            t = lax.dot_general(perm, a, NT_DIMS, preferred_element_type=F32)
            put(pl.ds(pl.multiple_of(k * 256, 256), 256), t.astype(BF16))
            return 0

        lax.fori_loop(0, 8, channel, 0)

    def u_copy(d):
        at = pl.multiple_of(lax.rem(y + NY - d, NY) * 128, 128)
        return pltpu.make_async_copy(ub.at[d], u_ref.at[:, pl.ds(at, 128), :], us.at[d])

    def turn_early(d):
        o = lax.broadcasted_iota(jnp.int32, (256, 256), 0)
        want = ((o >> 3) & 1) * 128 + ((o >> 4) & 7) * 16 + (o >> 7) * 8 + (o & 7)

        def put(lanes, t):
            ub[d, :, :, lanes] = t.reshape(2, 128, 256)

        turn_pair(d, want, put)
        u_copy(d).start()

    def turn_late():
        o = lax.broadcasted_iota(jnp.int32, (256, 256), 0)
        want = ((o >> 3) & 1) * 128 + (o >> 5) * 16 + ((o >> 4) & 1) * 8 + (o & 7)

        def put(lanes, t):
            zbuf[:, :, :, lanes] = t.reshape(NZ, 2, 16, 256)

        turn_pair(3, want, put)

    v_copy(pieces[0]).wait()
    prepare(0)
    pl.semaphore_wait(barrier, NY * NZ - 1 + NT - 1)
    send_step(0)
    v_copy(pieces[1]).wait()
    prepare(1)
    send_step(1)
    v_copy(pieces[2]).wait()
    v_copy(pieces[3]).wait()

    def prime_late(j, _):
        def put(lane, tile):
            recv[j, :, :, HIST + lane : HIST + lane + 512] = tile

        relayout(j, put)
        send_halo(j)
        return 0

    lax.fori_loop(FIRST, STEPS, prime_late, 0)

    taps_copy.wait()
    half = lax.broadcasted_iota(jnp.int32, (16, 128), 1) < CH
    taps = jnp.concatenate([taps_ref[...], taps_ref[...]], axis=1)
    ppad[...] = jnp.zeros_like(ppad)
    ppad[8:24, :] = jnp.where(half, taps, 0.0)
    ppad[9:25, :] = ppad[9:25, :] + jnp.where(half, 0.0, taps)
    for i in range(WIN // 128):
        tile = ppad[24 - 2 * i : 32 - 2 * i, :]
        t16[:, 128 * i : 128 * i + 128] = jnp.concatenate([tile, tile], axis=0)

    def weights(i, _):
        rows = pl.ds(pl.multiple_of(i * 16, 16), 16)
        sine = (i >= COS_ROWS // 16).astype(jnp.int32)
        r = i * 16 + lax.broadcasted_iota(jnp.int32, (16, 128), 0) - sine * COS_ROWS
        b = lax.broadcasted_iota(jnp.int32, (16, 128), 1)
        turn = ((r >> 3) * b - sine * (CH // 4)) & (CH - 1)
        trig = jnp.cos(turn.astype(F32) * (2 * math.pi / CH)) * (1 / math.sqrt(CH))
        for t in range(WIN // 128):
            lanes = slice(128 * t, 128 * t + 128)
            w = t16[:, lanes] * trig
            hi = w.astype(BF16)
            w_hi[rows, lanes] = hi
            w_lo[rows, lanes] = (w - hi.astype(F32)).astype(BF16)
        return 0

    lax.fori_loop(0, (COS_ROWS + SIN_ROWS) // 16, weights, 0)

    def step(i, _):
        j = jnp.where(i < 2, FIRST + i, i - 2)

        @pl.when(i >= 2)
        def _():
            @pl.when(j + AHEAD < FIRST)
            def _():
                prepare(j + AHEAD)
                send_step(j + AHEAD)

            @pl.when(j + AHEAD >= FIRST)
            def _():
                send_late(j + AHEAD)

            wait_step(j)
            send_halo(j)

        filterbank(j)

        @pl.when(j == LATE_AT)
        def _():
            turn_late()

        @pl.when((j == 3) | (j == 5))
        def _():
            turn_early(lax.div(j - 3, 2))

        return 0

    lax.fori_loop(0, STEPS, step, 0)
    turn_early(2)

    def finish(j, _):
        @pl.when(j < 2)
        def _():
            part = sb.at[j, pl.ds(0, NZ - 1)]
            pltpu.make_async_copy(part, part, zs.at[j]).wait()

        @pl.when(j >= 2)
        def _():
            part = sb.at[0]
            pltpu.make_async_copy(part, part, zs.at[j]).wait()

        @pl.when(tm < NT - 1)
        def _():
            halo_copy(j).wait_send()

        others = spec.at[j, :, pl.ds(0, 56)]
        pltpu.make_async_copy(others, others, xs.at[j]).wait()
        return 0

    lax.fori_loop(0, STEPS, finish, 0)
    for d in range(3):
        u_copy(d).wait()
    for j in range(FIRST, STEPS):
        wait_step(j)


LATE_AT = 1


def gram_kernel(u_ref, out_ref, held, sem):
    half = 256
    scale = 1.0 / 256

    def product(left, right):
        g = lax.dot_general(left, right, NT_DIMS, preferred_element_type=F32)
        return (g * scale).astype(BF16)

    copies = []

    def send(k, part, rows):
        c = pltpu.make_async_copy(
            held.at[k, part, rows], out_ref.at[0, k, part, rows], sem.at[len(copies)]
        )
        c.start()
        copies.append(c)

    top, bottom = pl.ds(0, half), pl.ds(half, half)
    for k in range(8):
        lanes = slice(256 * k, 256 * k + 256)
        re, im = u_ref[0, :, lanes], u_ref[1, :, lanes]
        u = jnp.concatenate([re, im], axis=1)
        w = jnp.concatenate([im, -re], axis=1)
        g = product(jnp.concatenate([u[:half], w[:half]], axis=0), u)
        held[k, 0, top] = g[:half]
        held[k, 1, top] = g[half:]
        send(k, 0, top)
        send(k, 1, top)
        held[k, 0, bottom, :half] = g[:half, half:].T
        held[k, 1, bottom, :half] = -(g[half:, half:].T)
        g = product(jnp.concatenate([u[half:], w[half:]], axis=0), u[half:])
        held[k, 0, bottom, half:] = g[:half]
        held[k, 1, bottom, half:] = g[half:]
        send(k, 0, bottom)
        send(k, 1, bottom)
    for c in copies:
        c.wait()


def body(voltages, fir_taps):
    dma = pltpu.SemaphoreType.DMA
    any_space = pl.BlockSpec(memory_space=pl.ANY)
    gathered = pl.pallas_call(
        comm_kernel,
        out_shape=jax.ShapeDtypeStruct((2, 512, 8 * 256), BF16),
        in_specs=[pl.BlockSpec(memory_space=pltpu.HBM)] * 2,
        out_specs=any_space,
        scratch_shapes=[
            pltpu.VMEM((4, 2, 8, 16, N), BF16),
            pltpu.VMEM((16, CH), F32),
            pltpu.VMEM((FIRST, NZ, ROWS, N), BF16),
            pltpu.VMEM((STEPS, NZ, ROWS, HIST + N), BF16),
            pltpu.VMEM((LANES, HIST + N), BF16),
            pltpu.VMEM((STEPS, 2, CH, 16, 128), BF16),
            pltpu.VMEM((STEPS, NT, 2, 8, 16, 128), BF16),
            pltpu.VMEM((3, 2, 128, 8 * 256), BF16),
            pltpu.VMEM((NZ, 2, 16, 8 * 256), BF16),
            pltpu.VMEM((COS_ROWS + SIN_ROWS, WIN), BF16),
            pltpu.VMEM((COS_ROWS + SIN_ROWS, WIN), BF16),
            pltpu.VMEM((32, 128), F32),
            pltpu.VMEM((16, WIN), F32),
            pltpu.VMEM((COS_ROWS, 256), F32),
            pltpu.VMEM((SIN_ROWS, 256), F32),
            dma((4,)),
            dma((1,)),
        ]
        + [dma((STEPS,))] * 6
        + [dma((3,))],
        compiler_params=pltpu.CompilerParams(
            collective_id=0, has_side_effects=True, vmem_limit_bytes=48 * 2**20
        ),
        name="exchange",
    )(voltages, fir_taps)
    return pl.pallas_call(
        gram_kernel,
        out_shape=jax.ShapeDtypeStruct((1, 8, 2, 512, 512), BF16),
        in_specs=[pl.BlockSpec(memory_space=pltpu.VMEM)],
        out_specs=any_space,
        scratch_shapes=[pltpu.VMEM((8, 2, 512, 512), BF16), dma((32,))],
        compiler_params=pltpu.CompilerParams(vmem_limit_bytes=24 * 2**20),
        name="gram",
    )(gathered)


def solution(mesh):
    return jax.shard_map(
        body,
        mesh=mesh,
        in_specs=(P(None, "stn", None, "tm"), P()),
        out_specs=P("stn", "tm", None, None, None),
        check_vma=False,
    )
```

```python
import functools
import math

import jax
import jax.numpy as jnp
from jax import lax
from jax.experimental import pallas as pl
from jax.experimental.pallas import tpu as pltpu
from jax.sharding import PartitionSpec as P

MESH = pl.DeviceIdType.MESH
F32 = jnp.float32
BF16 = jnp.bfloat16

NY, NZ, NT = 4, 8, 8
STEPS = 8
ROWS = 16
LANES = NZ * ROWS
N = 2048
HIST = 1024
WIN = 1536
CH = 64
COS_ROWS = 34 * 8
SIN_ROWS = 32 * 8
AHEAD = 2
FIRST = 6
ORDER = (1, 7, 2, 6, 3, 5, 4, 0)
NT_DIMS = (((1,), (1,)), ((), ()))


def comm_kernel(
    v_ref, taps_hbm, u_ref,
    vbuf, taps_ref, sb, recv, jx, spec, xg, ub, zbuf,
    w_hi, w_lo, ppad, t16, rc, rs,
    round_sem, v_sem, c_sem, zs, zr, hs, hr, xs, xr, us,
):
    stn = lax.axis_index("stn")
    tm = lax.axis_index("tm")
    y = lax.div(stn, NZ)
    z = lax.rem(stn, NZ)

    barrier = pltpu.get_barrier_semaphore()

    in_row = [(y * NZ + lax.rem(z + i, NZ), tm) for i in range(1, NZ)]
    in_column = [(lax.rem(y + i, NY) * NZ + z, tm) for i in range(1, NY)]
    sibling = [(stn, tm + 1 - 2 * lax.rem(tm, 2))]
    in_line = [(stn, lax.rem(tm + 2 * i, NT)) for i in range(1, NT // 2)]
    greeted = in_row + in_column + sibling + in_line
    crossed = in_column + in_line

    def v_copy(i):
        qt, h = lax.div(i, 2), lax.rem(i, 2)
        return pltpu.make_async_copy(
            v_ref.at[:, pl.ds(pl.multiple_of(h * 8, 8), 8), pl.ds(pl.multiple_of(qt * 16, 16), 16), :],
            vbuf.at[i],
            v_sem.at[i],
        )

    taps_copy = pltpu.make_async_copy(taps_hbm, taps_ref, c_sem.at[0])
    first = lax.div(y, 2) * 2
    pieces = (first, first + 1, 2 - first, 3 - first)
    for device in greeted:
        pl.semaphore_signal(barrier, inc=1, device_id=device, device_id_type=MESH)
    for i in pieces:
        v_copy(i).start()
    taps_copy.start()

    def relayout(j, put):
        d, h = lax.div(j, 2), lax.rem(j, 2)
        yt = lax.rem(y + d, NY)
        at = lax.div(yt, 2) * 2 + h
        odd = lax.rem(yt, 2)
        o = lax.broadcasted_iota(jnp.int32, (LANES, 256), 0)
        c = lax.broadcasted_iota(jnp.int32, (LANES, 256), 1)
        want = ((o >> 3) & 1) * 128 + (o & 7) * 16 + odd * 8 + (o >> 4)
        perm = jnp.where(c == want, 1.0, 0.0).astype(BF16)
        for lane in range(0, N, 512):
            x = vbuf[at, :, :, :, lane : lane + 512].reshape(256, 512)
            turned = jnp.dot(perm, x, preferred_element_type=F32).astype(BF16)
            put(lane, turned.reshape(NZ, ROWS, 512))

    def z_target(j, dz):
        zt = lax.rem(z + dz, NZ)
        yt = lax.rem(y + lax.div(j, 2), NY)
        return zt, (yt * NZ + zt, tm)

    def z_copy(j, dz):
        zt, to = z_target(j, dz)
        return pltpu.make_async_remote_copy(
            src_ref=sb.at[j, zt],
            dst_ref=recv.at[j, z, :, pl.ds(HIST, N)],
            send_sem=zs.at[j],
            recv_sem=zr.at[j],
            device_id=to,
            device_id_type=MESH,
        )

    def own_copy(j):
        return pltpu.make_async_copy(
            sb.at[j, z], recv.at[j, z, :, pl.ds(HIST, N)], zr.at[j]
        )

    def late_copy(j, dz):
        zt, to = z_target(j, dz)
        ri = lax.rem(j, 2)
        at = pl.multiple_of(y * 128 + z * 16, 16)
        return pltpu.make_async_remote_copy(
            src_ref=zbuf.at[zt, ri],
            dst_ref=u_ref.at[ri, pl.ds(at, 16), :],
            send_sem=zs.at[j],
            recv_sem=zr.at[j],
            device_id=to,
            device_id_type=MESH,
        )

    def prepare(j):
        def put(lane, tile):
            sb[j, :, :, lane : lane + 512] = tile

        relayout(j, put)

    def send_step(j):
        for dz in ORDER[:-1]:
            z_copy(j, dz).start()

        @pl.when(j < 2)
        def _():
            own_copy(j).start()

        @pl.when(j >= 2)
        def _():
            z_copy(j, 0).start()

    def send_late(j):
        for dz in ORDER:
            late_copy(j, dz).start()

    def wait_step(j):
        whole = recv.at[j, :, :, pl.ds(HIST, N)]
        pltpu.make_async_copy(whole, whole, zr.at[j]).wait()

    def halo_copy(j):
        return pltpu.make_async_remote_copy(
            src_ref=recv.at[j, :, :, pl.ds(N, HIST)],
            dst_ref=recv.at[j, :, :, pl.ds(0, HIST)],
            send_sem=hs.at[j],
            recv_sem=hr.at[j],
            device_id=(stn, lax.rem(tm + 1, NT)),
            device_id_type=MESH,
        )

    def send_halo(j):
        @pl.when(tm < NT - 1)
        def _():
            halo_copy(j).start()

    def wait_halo(j):
        @pl.when(tm > 0)
        def _():
            halo_copy(j).wait_recv()

        @pl.when(tm == 0)
        def _():
            recv[j, :, :, 0:HIST] = jnp.zeros((NZ, ROWS, HIST), BF16)

    def x_copy(j, gp, o):
        to = lax.rem(tm + o, NT)
        return pltpu.make_async_remote_copy(
            src_ref=spec.at[j, gp, pl.ds(to * 8, 8)],
            dst_ref=xg.at[j, tm, gp],
            send_sem=xs.at[j],
            recv_sem=xr.at[j],
            device_id=(stn, to),
            device_id_type=MESH,
        )

    def x_own(j, gp):
        return pltpu.make_async_copy(
            spec.at[j, gp, pl.ds(tm * 8, 8)], xg.at[j, tm, gp], xr.at[j]
        )

    def turn_complex(j, lane):
        o = lax.broadcasted_iota(jnp.int32, (LANES, LANES), 0)
        c = lax.broadcasted_iota(jnp.int32, (LANES, LANES), 1)
        im = (o >> 3) & 1
        sign = (1 - 2 * im).astype(F32)
        turn = jnp.where(c == o + 8 - 16 * im, sign, 0.0).astype(BF16)
        x = recv[j, :, :, lane : lane + 512].reshape(LANES, 512)
        jx[:, lane : lane + 512] = jnp.dot(turn, x, preferred_element_type=F32).astype(BF16)

    def spectra(j, gp):
        lo0 = 1024 * gp
        lo1 = lo0 + 512

        def both(w0, w1, x):
            hi = lax.dot_general(w_hi[w0:w1, :], x, NT_DIMS, preferred_element_type=F32)
            lo = lax.dot_general(w_lo[w0:w1, :], x, NT_DIMS, preferred_element_type=F32)
            return hi + lo

        x = jnp.concatenate(
            [
                recv[j, :, :, lo0 : lo0 + WIN].reshape(LANES, WIN),
                recv[j, :, :, lo1 : lo1 + WIN].reshape(LANES, WIN),
            ],
            axis=0,
        )
        rc[...] = both(0, COS_ROWS, x)
        x = jnp.concatenate([jx[:, lo0 : lo0 + WIN], jx[:, lo1 : lo1 + WIN]], axis=0)
        rs[...] = both(COS_ROWS, COS_ROWS + SIN_ROWS, x)

        def put(k, a):
            tile = jnp.concatenate([a[:, :128], a[:, 128:]], axis=0)
            spec[j, gp, k] = tile.astype(BF16)

        put(0, rc[0:8, :])
        put(32, rc[256:264, :])
        for k in range(1, 32):
            c = rc[8 * k : 8 * k + 8, :]
            s = rs[8 * k : 8 * k + 8, :]
            put(k, c + s)
            put(64 - k, c - s)

    def send_spectra(j, gp):
        def start(o, _):
            x_copy(j, gp, o).start()
            return 0

        lax.fori_loop(1, NT, start, 0)
        x_own(j, gp).start()

    def filterbank(j):
        for lane in range(HIST, HIST + N, 512):
            turn_complex(j, lane)
        spectra(j, 1)
        send_spectra(j, 1)
        wait_halo(j)
        for lane in range(0, HIST, 512):
            turn_complex(j, lane)
        spectra(j, 0)
        send_spectra(j, 0)

    def wait_spectra(j):
        pltpu.make_async_copy(spec.at[j], spec.at[j], xr.at[j]).wait()

    def turn_pair(d, want, put):
        wait_spectra(2 * d)
        wait_spectra(2 * d + 1)
        c = lax.broadcasted_iota(jnp.int32, (256, 256), 1)
        perm = jnp.where(c == want, 1.0, 0.0).astype(BF16)

        def channel(k, _):
            a = jnp.concatenate(
                [
                    xg[2 * d, :, :, k].reshape(256, LANES),
                    xg[2 * d + 1, :, :, k].reshape(256, LANES),
                ],
                axis=1,
            )
            t = lax.dot_general(perm, a, NT_DIMS, preferred_element_type=F32)
            put(pl.ds(pl.multiple_of(k * 256, 256), 256), t.astype(BF16))
            return 0

        lax.fori_loop(0, 8, channel, 0)

    def u_copy(d):
        at = pl.multiple_of(lax.rem(y + NY - d, NY) * 128, 128)
        return pltpu.make_async_copy(ub.at[d], u_ref.at[:, pl.ds(at, 128), :], us.at[d])

    def turn_early(d):
        o = lax.broadcasted_iota(jnp.int32, (256, 256), 0)
        want = ((o >> 3) & 1) * 128 + ((o >> 4) & 7) * 16 + (o >> 7) * 8 + (o & 7)

        def put(lanes, t):
            ub[d, :, :, lanes] = t.reshape(2, 128, 256)

        turn_pair(d, want, put)
        u_copy(d).start()

    def turn_late():
        o = lax.broadcasted_iota(jnp.int32, (256, 256), 0)
        want = ((o >> 3) & 1) * 128 + (o >> 5) * 16 + ((o >> 4) & 1) * 8 + (o & 7)

        def put(lanes, t):
            zbuf[:, :, :, lanes] = t.reshape(NZ, 2, 16, 256)

        turn_pair(3, want, put)

    v_copy(pieces[0]).wait()
    prepare(0)
    pl.semaphore_wait(barrier, len(greeted))
    send_step(0)
    for device in crossed:
        pl.semaphore_signal(round_sem, inc=1, device_id=device, device_id_type=MESH)
    v_copy(pieces[1]).wait()
    prepare(1)
    send_step(1)
    pl.semaphore_wait(round_sem, len(crossed))
    v_copy(pieces[2]).wait()
    v_copy(pieces[3]).wait()

    def prime_late(j, _):
        def put(lane, tile):
            recv[j, :, :, HIST + lane : HIST + lane + 512] = tile

        relayout(j, put)
        send_halo(j)
        return 0

    lax.fori_loop(FIRST, STEPS, prime_late, 0)

    taps_copy.wait()
    half = lax.broadcasted_iota(jnp.int32, (16, 128), 1) < CH
    taps = jnp.concatenate([taps_ref[...], taps_ref[...]], axis=1)
    ppad[...] = jnp.zeros_like(ppad)
    ppad[8:24, :] = jnp.where(half, taps, 0.0)
    ppad[9:25, :] = ppad[9:25, :] + jnp.where(half, 0.0, taps)
    for i in range(WIN // 128):
        tile = ppad[24 - 2 * i : 32 - 2 * i, :]
        t16[:, 128 * i : 128 * i + 128] = jnp.concatenate([tile, tile], axis=0)

    def weights(i, _):
        rows = pl.ds(pl.multiple_of(i * 16, 16), 16)
        sine = (i >= COS_ROWS // 16).astype(jnp.int32)
        r = i * 16 + lax.broadcasted_iota(jnp.int32, (16, 128), 0) - sine * COS_ROWS
        b = lax.broadcasted_iota(jnp.int32, (16, 128), 1)
        turn = ((r >> 3) * b - sine * (CH // 4)) & (CH - 1)
        trig = jnp.cos(turn.astype(F32) * (2 * math.pi / CH)) * (1 / math.sqrt(CH))
        for t in range(WIN // 128):
            lanes = slice(128 * t, 128 * t + 128)
            w = t16[:, lanes] * trig
            hi = w.astype(BF16)
            w_hi[rows, lanes] = hi
            w_lo[rows, lanes] = (w - hi.astype(F32)).astype(BF16)
        return 0

    lax.fori_loop(0, (COS_ROWS + SIN_ROWS) // 16, weights, 0)

    def step(i, _):
        j = jnp.where(i < 2, FIRST + i, i - 2)

        @pl.when(i >= 2)
        def _():
            @pl.when(j + AHEAD < FIRST)
            def _():
                prepare(j + AHEAD)
                send_step(j + AHEAD)

            @pl.when(j + AHEAD >= FIRST)
            def _():
                send_late(j + AHEAD)

            wait_step(j)
            send_halo(j)

        filterbank(j)

        @pl.when(j == LATE_AT)
        def _():
            turn_late()

        @pl.when((j == 3) | (j == 5))
        def _():
            turn_early(lax.div(j - 3, 2))

        return 0

    lax.fori_loop(0, STEPS, step, 0)
    turn_early(2)

    def finish(j, _):
        @pl.when(j < 2)
        def _():
            part = sb.at[j, pl.ds(0, NZ - 1)]
            pltpu.make_async_copy(part, part, zs.at[j]).wait()

        @pl.when(j >= 2)
        def _():
            part = sb.at[0]
            pltpu.make_async_copy(part, part, zs.at[j]).wait()

        @pl.when(tm < NT - 1)
        def _():
            halo_copy(j).wait_send()

        others = spec.at[j, :, pl.ds(0, 56)]
        pltpu.make_async_copy(others, others, xs.at[j]).wait()
        return 0

    lax.fori_loop(0, STEPS, finish, 0)
    for d in range(3):
        u_copy(d).wait()
    for j in range(FIRST, STEPS):
        wait_step(j)


LATE_AT = 1


def gram_kernel(u_ref, out_ref, held, sem):
    half = 256
    scale = 1.0 / 256

    def product(left, right):
        g = lax.dot_general(left, right, NT_DIMS, preferred_element_type=F32)
        return (g * scale).astype(BF16)

    copies = []

    def send(k, part, rows):
        c = pltpu.make_async_copy(
            held.at[k, part, rows], out_ref.at[0, k, part, rows], sem.at[len(copies)]
        )
        c.start()
        copies.append(c)

    top, bottom = pl.ds(0, half), pl.ds(half, half)
    for k in range(8):
        lanes = slice(256 * k, 256 * k + 256)
        re, im = u_ref[0, :, lanes], u_ref[1, :, lanes]
        u = jnp.concatenate([re, im], axis=1)
        w = jnp.concatenate([im, -re], axis=1)
        g = product(jnp.concatenate([u[:half], w[:half]], axis=0), u)
        held[k, 0, top] = g[:half]
        held[k, 1, top] = g[half:]
        send(k, 0, top)
        send(k, 1, top)
        held[k, 0, bottom, :half] = g[:half, half:].T
        held[k, 1, bottom, :half] = -(g[half:, half:].T)
        g = product(jnp.concatenate([u[half:], w[half:]], axis=0), u[half:])
        held[k, 0, bottom, half:] = g[:half]
        held[k, 1, bottom, half:] = g[half:]
        send(k, 0, bottom)
        send(k, 1, bottom)
    for c in copies:
        c.wait()


def body(voltages, fir_taps):
    dma = pltpu.SemaphoreType.DMA
    any_space = pl.BlockSpec(memory_space=pl.ANY)
    gathered = pl.pallas_call(
        comm_kernel,
        out_shape=jax.ShapeDtypeStruct((2, 512, 8 * 256), BF16),
        in_specs=[pl.BlockSpec(memory_space=pltpu.HBM)] * 2,
        out_specs=any_space,
        scratch_shapes=[
            pltpu.VMEM((4, 2, 8, 16, N), BF16),
            pltpu.VMEM((16, CH), F32),
            pltpu.VMEM((FIRST, NZ, ROWS, N), BF16),
            pltpu.VMEM((STEPS, NZ, ROWS, HIST + N), BF16),
            pltpu.VMEM((LANES, HIST + N), BF16),
            pltpu.VMEM((STEPS, 2, CH, 16, 128), BF16),
            pltpu.VMEM((STEPS, NT, 2, 8, 16, 128), BF16),
            pltpu.VMEM((3, 2, 128, 8 * 256), BF16),
            pltpu.VMEM((NZ, 2, 16, 8 * 256), BF16),
            pltpu.VMEM((COS_ROWS + SIN_ROWS, WIN), BF16),
            pltpu.VMEM((COS_ROWS + SIN_ROWS, WIN), BF16),
            pltpu.VMEM((32, 128), F32),
            pltpu.VMEM((16, WIN), F32),
            pltpu.VMEM((COS_ROWS, 256), F32),
            pltpu.VMEM((SIN_ROWS, 256), F32),
            pltpu.SemaphoreType.REGULAR,
            dma((4,)),
            dma((1,)),
        ]
        + [dma((STEPS,))] * 6
        + [dma((3,))],
        compiler_params=pltpu.CompilerParams(
            collective_id=0, has_side_effects=True, vmem_limit_bytes=48 * 2**20
        ),
        name="exchange",
    )(voltages, fir_taps)
    return pl.pallas_call(
        gram_kernel,
        out_shape=jax.ShapeDtypeStruct((1, 8, 2, 512, 512), BF16),
        in_specs=[pl.BlockSpec(memory_space=pltpu.VMEM)],
        out_specs=any_space,
        scratch_shapes=[pltpu.VMEM((8, 2, 512, 512), BF16), dma((32,))],
        compiler_params=pltpu.CompilerParams(vmem_limit_bytes=24 * 2**20),
        name="gram",
    )(gathered)


def solution(mesh):
    return jax.shard_map(
        body,
        mesh=mesh,
        in_specs=(P(None, "stn", None, "tm"), P()),
        out_specs=P("stn", "tm", None, None, None),
        check_vma=False,
    )
```

```python
import functools
import math

import jax
import jax.numpy as jnp
from jax import lax
from jax.experimental import pallas as pl
from jax.experimental.pallas import tpu as pltpu
from jax.sharding import PartitionSpec as P

MESH = pl.DeviceIdType.MESH
F32 = jnp.float32
BF16 = jnp.bfloat16

NY, NZ, NT = 4, 8, 8
STEPS = 8
ROWS = 16
LANES = NZ * ROWS
N = 2048
HIST = 1024
WIN = 1536
CH = 64
COS_ROWS = 34 * 8
SIN_ROWS = 32 * 8
AHEAD = 2
FIRST = 6
ORDER = (1, 7, 2, 6, 3, 5, 4, 0)
NT_DIMS = (((1,), (1,)), ((), ()))


def comm_kernel(
    v_ref, taps_hbm, u_ref, g_ref,
    vbuf, taps_ref, sb, recv, jx, spec, xg, ua, ub, zbuf, gbuf,
    w_hi, w_lo, ppad, t16, rc, rs,
    round_sem, v_sem, c_sem, zs, zr, hs, hr, xs, xr, us, gs,
):
    stn = lax.axis_index("stn")
    tm = lax.axis_index("tm")
    y = lax.div(stn, NZ)
    z = lax.rem(stn, NZ)

    barrier = pltpu.get_barrier_semaphore()

    in_row = [(y * NZ + lax.rem(z + i, NZ), tm) for i in range(1, NZ)]
    in_column = [(lax.rem(y + i, NY) * NZ + z, tm) for i in range(1, NY)]
    sibling = [(stn, tm + 1 - 2 * lax.rem(tm, 2))]
    in_line = [(stn, lax.rem(tm + 2 * i, NT)) for i in range(1, NT // 2)]
    greeted = in_row + in_column + sibling + in_line
    crossed = in_column + in_line

    def v_copy(i):
        qt, h = lax.div(i, 2), lax.rem(i, 2)
        return pltpu.make_async_copy(
            v_ref.at[:, pl.ds(pl.multiple_of(h * 8, 8), 8), pl.ds(pl.multiple_of(qt * 16, 16), 16), :],
            vbuf.at[i],
            v_sem.at[i],
        )

    taps_copy = pltpu.make_async_copy(taps_hbm, taps_ref, c_sem.at[0])
    first = lax.div(y, 2) * 2
    pieces = (first, first + 1, 2 - first, 3 - first)
    for device in greeted:
        pl.semaphore_signal(barrier, inc=1, device_id=device, device_id_type=MESH)
    for i in pieces:
        v_copy(i).start()
    taps_copy.start()

    def relayout(j, put):
        d, h = lax.div(j, 2), lax.rem(j, 2)
        yt = lax.rem(y + d, NY)
        at = lax.div(yt, 2) * 2 + h
        odd = lax.rem(yt, 2)
        o = lax.broadcasted_iota(jnp.int32, (LANES, 256), 0)
        c = lax.broadcasted_iota(jnp.int32, (LANES, 256), 1)
        want = ((o >> 3) & 1) * 128 + (o & 7) * 16 + odd * 8 + (o >> 4)
        perm = jnp.where(c == want, 1.0, 0.0).astype(BF16)
        for lane in range(0, N, 512):
            x = vbuf[at, :, :, :, lane : lane + 512].reshape(256, 512)
            turned = jnp.dot(perm, x, preferred_element_type=F32).astype(BF16)
            put(lane, turned.reshape(NZ, ROWS, 512))

    def z_target(j, dz):
        zt = lax.rem(z + dz, NZ)
        yt = lax.rem(y + lax.div(j, 2), NY)
        return zt, (yt * NZ + zt, tm)

    def z_copy(j, dz):
        zt, to = z_target(j, dz)
        return pltpu.make_async_remote_copy(
            src_ref=sb.at[j, zt],
            dst_ref=recv.at[j, z, :, pl.ds(HIST, N)],
            send_sem=zs.at[j],
            recv_sem=zr.at[j],
            device_id=to,
            device_id_type=MESH,
        )

    def own_copy(j):
        return pltpu.make_async_copy(
            sb.at[j, z], recv.at[j, z, :, pl.ds(HIST, N)], zr.at[j]
        )

    def late_copy(j, dz):
        zt, to = z_target(j, dz)
        target = ua if j == FIRST else u_ref
        at = pl.multiple_of(y * 128 + z * 16, 16)
        return pltpu.make_async_remote_copy(
            src_ref=zbuf.at[zt, j - FIRST],
            dst_ref=target.at[:, pl.ds(at, 16), :],
            send_sem=zs.at[j],
            recv_sem=zr.at[j],
            device_id=to,
            device_id_type=MESH,
        )

    def prepare(j):
        def put(lane, tile):
            sb[j, :, :, lane : lane + 512] = tile

        relayout(j, put)

    def send_step(j):
        for dz in ORDER[:-1]:
            z_copy(j, dz).start()

        @pl.when(j < 2)
        def _():
            own_copy(j).start()

        @pl.when(j >= 2)
        def _():
            z_copy(j, 0).start()

    def send_late(j):
        for dz in ORDER:
            late_copy(j, dz).start()

    def wait_step(j):
        whole = recv.at[j, :, :, pl.ds(HIST, N)]
        pltpu.make_async_copy(whole, whole, zr.at[j]).wait()

    def halo_copy(j):
        return pltpu.make_async_remote_copy(
            src_ref=recv.at[j, :, :, pl.ds(N, HIST)],
            dst_ref=recv.at[j, :, :, pl.ds(0, HIST)],
            send_sem=hs.at[j],
            recv_sem=hr.at[j],
            device_id=(stn, lax.rem(tm + 1, NT)),
            device_id_type=MESH,
        )

    def send_halo(j):
        @pl.when(tm < NT - 1)
        def _():
            halo_copy(j).start()

    def wait_halo(j):
        @pl.when(tm > 0)
        def _():
            halo_copy(j).wait_recv()

        @pl.when(tm == 0)
        def _():
            recv[j, :, :, 0:HIST] = jnp.zeros((NZ, ROWS, HIST), BF16)

    def x_copy(j, gp, o):
        to = lax.rem(tm + o, NT)
        return pltpu.make_async_remote_copy(
            src_ref=spec.at[j, gp, pl.ds(to * 8, 8)],
            dst_ref=xg.at[j, tm, gp],
            send_sem=xs.at[j],
            recv_sem=xr.at[j],
            device_id=(stn, to),
            device_id_type=MESH,
        )

    def x_own(j, gp):
        return pltpu.make_async_copy(
            spec.at[j, gp, pl.ds(tm * 8, 8)], xg.at[j, tm, gp], xr.at[j]
        )

    def turn_complex(j, lane):
        o = lax.broadcasted_iota(jnp.int32, (LANES, LANES), 0)
        c = lax.broadcasted_iota(jnp.int32, (LANES, LANES), 1)
        im = (o >> 3) & 1
        sign = (1 - 2 * im).astype(F32)
        turn = jnp.where(c == o + 8 - 16 * im, sign, 0.0).astype(BF16)
        x = recv[j, :, :, lane : lane + 512].reshape(LANES, 512)
        jx[:, lane : lane + 512] = jnp.dot(turn, x, preferred_element_type=F32).astype(BF16)

    def spectra(j, gp):
        lo0 = 1024 * gp
        lo1 = lo0 + 512

        def both(w0, w1, x):
            hi = lax.dot_general(w_hi[w0:w1, :], x, NT_DIMS, preferred_element_type=F32)
            lo = lax.dot_general(w_lo[w0:w1, :], x, NT_DIMS, preferred_element_type=F32)
            return hi + lo

        x = jnp.concatenate(
            [
                recv[j, :, :, lo0 : lo0 + WIN].reshape(LANES, WIN),
                recv[j, :, :, lo1 : lo1 + WIN].reshape(LANES, WIN),
            ],
            axis=0,
        )
        rc[...] = both(0, COS_ROWS, x)
        x = jnp.concatenate([jx[:, lo0 : lo0 + WIN], jx[:, lo1 : lo1 + WIN]], axis=0)
        rs[...] = both(COS_ROWS, COS_ROWS + SIN_ROWS, x)

        def put(k, a):
            tile = jnp.concatenate([a[:, :128], a[:, 128:]], axis=0)
            spec[j, gp, k] = tile.astype(BF16)

        put(0, rc[0:8, :])
        put(32, rc[256:264, :])
        for k in range(1, 32):
            c = rc[8 * k : 8 * k + 8, :]
            s = rs[8 * k : 8 * k + 8, :]
            put(k, c + s)
            put(64 - k, c - s)

    def send_spectra(j, gp):
        def start(o, _):
            x_copy(j, gp, o).start()
            return 0

        lax.fori_loop(1, NT, start, 0)
        x_own(j, gp).start()

    def filterbank(j):
        for lane in range(HIST, HIST + N, 512):
            turn_complex(j, lane)
        spectra(j, 1)
        send_spectra(j, 1)
        wait_halo(j)
        for lane in range(0, HIST, 512):
            turn_complex(j, lane)
        spectra(j, 0)
        send_spectra(j, 0)

    def wait_spectra(j):
        pltpu.make_async_copy(spec.at[j], spec.at[j], xr.at[j]).wait()

    def turn_pair(d, want, put, put_rest):
        wait_spectra(2 * d)
        wait_spectra(2 * d + 1)
        c = lax.broadcasted_iota(jnp.int32, (256, 256), 1)
        perm = jnp.where(c == want, 1.0, 0.0).astype(BF16)

        def channel(k, store):
            a = jnp.concatenate(
                [
                    xg[2 * d, :, :, k].reshape(256, LANES),
                    xg[2 * d + 1, :, :, k].reshape(256, LANES),
                ],
                axis=1,
            )
            t = lax.dot_general(perm, a, NT_DIMS, preferred_element_type=F32)
            lanes = pl.ds(pl.multiple_of((k % 4) * 256, 256), 256)
            store(lanes, t.astype(BF16))

        def early(k, _):
            channel(k, put)
            return 0

        def rest(k, _):
            channel(k, put_rest)
            return 0

        lax.fori_loop(0, 4, early, 0)
        lax.fori_loop(4, 8, rest, 0)

    def rows_of(d):
        return pl.ds(pl.multiple_of(lax.rem(y + NY - d, NY) * 128, 128), 128)

    def u_copy(d):
        return pltpu.make_async_copy(ub.at[d], u_ref.at[:, rows_of(d), :], us.at[d])

    def turn_early(d):
        o = lax.broadcasted_iota(jnp.int32, (256, 256), 0)
        want = ((o >> 3) & 1) * 128 + ((o >> 4) & 7) * 16 + (o >> 7) * 8 + (o & 7)

        def put(lanes, t):
            ua[:, rows_of(d), lanes] = t.reshape(2, 128, 256)

        def put_rest(lanes, t):
            ub[d, :, :, lanes] = t.reshape(2, 128, 256)

        turn_pair(d, want, put, put_rest)
        u_copy(d).start()

    def turn_late():
        o = lax.broadcasted_iota(jnp.int32, (256, 256), 0)
        want = ((o >> 3) & 1) * 128 + (o >> 5) * 16 + ((o >> 4) & 1) * 8 + (o & 7)

        def put(lanes, t):
            zbuf[:, 0, :, :, lanes] = t.reshape(NZ, 2, 16, 256)

        def put_rest(lanes, t):
            zbuf[:, 1, :, :, lanes] = t.reshape(NZ, 2, 16, 256)

        turn_pair(3, want, put, put_rest)

    v_copy(pieces[0]).wait()
    prepare(0)
    pl.semaphore_wait(barrier, len(greeted))
    send_step(0)
    for device in crossed:
        pl.semaphore_signal(round_sem, inc=1, device_id=device, device_id_type=MESH)
    v_copy(pieces[1]).wait()
    prepare(1)
    send_step(1)
    pl.semaphore_wait(round_sem, len(crossed))
    v_copy(pieces[2]).wait()
    v_copy(pieces[3]).wait()

    def prime_late(j, _):
        def put(lane, tile):
            recv[j, :, :, HIST + lane : HIST + lane + 512] = tile

        relayout(j, put)
        send_halo(j)
        return 0

    lax.fori_loop(FIRST, STEPS, prime_late, 0)

    taps_copy.wait()
    half = lax.broadcasted_iota(jnp.int32, (16, 128), 1) < CH
    taps = jnp.concatenate([taps_ref[...], taps_ref[...]], axis=1)
    ppad[...] = jnp.zeros_like(ppad)
    ppad[8:24, :] = jnp.where(half, taps, 0.0)
    ppad[9:25, :] = ppad[9:25, :] + jnp.where(half, 0.0, taps)
    for i in range(WIN // 128):
        tile = ppad[24 - 2 * i : 32 - 2 * i, :]
        t16[:, 128 * i : 128 * i + 128] = jnp.concatenate([tile, tile], axis=0)

    def weights(i, _):
        rows = pl.ds(pl.multiple_of(i * 16, 16), 16)
        sine = (i >= COS_ROWS // 16).astype(jnp.int32)
        r = i * 16 + lax.broadcasted_iota(jnp.int32, (16, 128), 0) - sine * COS_ROWS
        b = lax.broadcasted_iota(jnp.int32, (16, 128), 1)
        turn = ((r >> 3) * b - sine * (CH // 4)) & (CH - 1)
        trig = jnp.cos(turn.astype(F32) * (2 * math.pi / CH)) * (1 / math.sqrt(CH))
        for t in range(WIN // 128):
            lanes = slice(128 * t, 128 * t + 128)
            w = t16[:, lanes] * trig
            hi = w.astype(BF16)
            w_hi[rows, lanes] = hi
            w_lo[rows, lanes] = (w - hi.astype(F32)).astype(BF16)
        return 0

    lax.fori_loop(0, (COS_ROWS + SIN_ROWS) // 16, weights, 0)

    def step(i, _):
        j = jnp.where(i < 2, FIRST + i, i - 2)

        @pl.when(i >= 2)
        def _():
            @pl.when(j + AHEAD < FIRST)
            def _():
                prepare(j + AHEAD)
                send_step(j + AHEAD)

            for late in range(FIRST, STEPS):
                @pl.when(j + AHEAD == late)
                def _(late=late):
                    send_late(late)

            wait_step(j)
            send_halo(j)

        filterbank(j)

        @pl.when(j == LATE_AT)
        def _():
            turn_late()

        @pl.when((j == 3) | (j == 5))
        def _():
            turn_early(lax.div(j - 3, 2))

        return 0

    lax.fori_loop(0, STEPS, step, 0)
    turn_early(2)

    def g_copy(k):
        return pltpu.make_async_copy(gbuf.at[k], g_ref.at[k], gs.at[k])

    wait_step(FIRST)

    def make_gram(k, _):
        lanes = pl.ds(pl.multiple_of(k * 256, 256), 256)
        gram_into(gbuf.at[k], ua[0, :, lanes], ua[1, :, lanes])
        g_copy(k).start()
        return 0

    lax.fori_loop(0, 4, make_gram, 0)

    def finish(j, _):
        @pl.when(j < 2)
        def _():
            part = sb.at[j, pl.ds(0, NZ - 1)]
            pltpu.make_async_copy(part, part, zs.at[j]).wait()

        @pl.when(j >= 2)
        def _():
            part = sb.at[0]
            pltpu.make_async_copy(part, part, zs.at[j]).wait()

        @pl.when(tm < NT - 1)
        def _():
            halo_copy(j).wait_send()

        others = spec.at[j, :, pl.ds(0, 56)]
        pltpu.make_async_copy(others, others, xs.at[j]).wait()
        return 0

    lax.fori_loop(0, STEPS, finish, 0)
    for d in range(3):
        u_copy(d).wait()
    for k in range(4):
        g_copy(k).wait()
    wait_step(STEPS - 1)


LATE_AT = 1


def gram_into(to, re, im, sent=lambda part, rows: None):
    half = 256
    top, bottom = slice(0, half), slice(half, 2 * half)

    def product(left, right):
        g = lax.dot_general(left, right, NT_DIMS, preferred_element_type=F32)
        return (g * (1.0 / 256)).astype(BF16)

    u = jnp.concatenate([re, im], axis=1)
    w = jnp.concatenate([im, -re], axis=1)
    g = product(jnp.concatenate([u[top], w[top]], axis=0), u)
    to[0, top, :] = g[top]
    to[1, top, :] = g[bottom]
    sent(0, pl.ds(0, half))
    sent(1, pl.ds(0, half))
    to[0, bottom, top] = g[top, bottom].T
    to[1, bottom, top] = -(g[bottom, bottom].T)
    g = product(jnp.concatenate([u[bottom], w[bottom]], axis=0), u[bottom])
    to[0, bottom, bottom] = g[top]
    to[1, bottom, bottom] = g[bottom]
    sent(0, pl.ds(half, half))
    sent(1, pl.ds(half, half))


def gram_kernel(u_ref, g_ref, out_ref, held, g_sem, sem):
    copies = [
        pltpu.make_async_copy(g_ref.at[k], out_ref.at[0, k], g_sem.at[k]) for k in range(4)
    ]
    for c in copies:
        c.start()
    for k in range(4):
        lanes = slice(256 * k, 256 * k + 256)

        def sent(part, rows, k=k):
            c = pltpu.make_async_copy(
                held.at[k, part, rows],
                out_ref.at[0, k + 4, part, rows],
                sem.at[len(copies) - 4],
            )
            c.start()
            copies.append(c)

        gram_into(held.at[k], u_ref[0, :, lanes], u_ref[1, :, lanes], sent)
    for c in copies:
        c.wait()


def body(voltages, fir_taps):
    dma = pltpu.SemaphoreType.DMA
    any_space = pl.BlockSpec(memory_space=pl.ANY)
    u, g = pl.pallas_call(
        comm_kernel,
        out_shape=[
            jax.ShapeDtypeStruct((2, 512, 4 * 256), BF16),
            jax.ShapeDtypeStruct((4, 2, 512, 512), BF16),
        ],
        in_specs=[pl.BlockSpec(memory_space=pltpu.HBM)] * 2,
        out_specs=[any_space, any_space],
        scratch_shapes=[
            pltpu.VMEM((4, 2, 8, 16, N), BF16),
            pltpu.VMEM((16, CH), F32),
            pltpu.VMEM((FIRST, NZ, ROWS, N), BF16),
            pltpu.VMEM((STEPS, NZ, ROWS, HIST + N), BF16),
            pltpu.VMEM((LANES, HIST + N), BF16),
            pltpu.VMEM((STEPS, 2, CH, 16, 128), BF16),
            pltpu.VMEM((STEPS, NT, 2, 8, 16, 128), BF16),
            pltpu.VMEM((2, 512, 4 * 256), BF16),
            pltpu.VMEM((3, 2, 128, 4 * 256), BF16),
            pltpu.VMEM((NZ, 2, 2, 16, 4 * 256), BF16),
            pltpu.VMEM((4, 2, 512, 512), BF16),
            pltpu.VMEM((COS_ROWS + SIN_ROWS, WIN), BF16),
            pltpu.VMEM((COS_ROWS + SIN_ROWS, WIN), BF16),
            pltpu.VMEM((32, 128), F32),
            pltpu.VMEM((16, WIN), F32),
            pltpu.VMEM((COS_ROWS, 256), F32),
            pltpu.VMEM((SIN_ROWS, 256), F32),
            pltpu.SemaphoreType.REGULAR,
            dma((4,)),
            dma((1,)),
        ]
        + [dma((STEPS,))] * 6
        + [dma((3,)), dma((4,))],
        compiler_params=pltpu.CompilerParams(
            collective_id=0, has_side_effects=True, vmem_limit_bytes=44 * 2**20
        ),
        name="exchange",
    )(voltages, fir_taps)
    return pl.pallas_call(
        gram_kernel,
        out_shape=jax.ShapeDtypeStruct((1, 8, 2, 512, 512), BF16),
        in_specs=[pl.BlockSpec(memory_space=pltpu.VMEM), any_space],
        out_specs=any_space,
        scratch_shapes=[pltpu.VMEM((4, 2, 512, 512), BF16), dma((4,)), dma((16,))],
        compiler_params=pltpu.CompilerParams(vmem_limit_bytes=24 * 2**20),
        name="gram",
    )(u, g)


def solution(mesh):
    return jax.shard_map(
        body,
        mesh=mesh,
        in_specs=(P(None, "stn", None, "tm"), P()),
        out_specs=P("stn", "tm", None, None, None),
        check_vma=False,
    )
```

```python
import functools
import math

import jax
import jax.numpy as jnp
from jax import lax
from jax.experimental import pallas as pl
from jax.experimental.pallas import tpu as pltpu
from jax.sharding import PartitionSpec as P

MESH = pl.DeviceIdType.MESH
F32 = jnp.float32
BF16 = jnp.bfloat16

NY, NZ, NT = 4, 8, 8
STEPS = 8
ROWS = 16
LANES = NZ * ROWS
N = 2048
HIST = 1024
WIN = 1536
CH = 64
COS_ROWS = 34 * 8
SIN_ROWS = 32 * 8
AHEAD = 2
FIRST = 6
ORDER = (1, 7, 2, 6, 3, 5, 4, 0)
NT_DIMS = (((1,), (1,)), ((), ()))


def comm_kernel(
    v_ref, taps_hbm, u_ref, g_ref,
    vbuf, taps_ref, sb, recv, jx, spec, xg, ua, ub, zbuf, gbuf,
    w_hi, w_lo, ppad, t16, rc, rs,
    round_sem, v_sem, c_sem, zs, zr, hs, hr, xs, xr, us, gs,
):
    stn = lax.axis_index("stn")
    tm = lax.axis_index("tm")
    y = lax.div(stn, NZ)
    z = lax.rem(stn, NZ)

    barrier = pltpu.get_barrier_semaphore()

    in_row = [(y * NZ + lax.rem(z + i, NZ), tm) for i in range(1, NZ)]
    in_column = [(lax.rem(y + i, NY) * NZ + z, tm) for i in range(1, NY)]
    sibling = [(stn, tm + 1 - 2 * lax.rem(tm, 2))]
    in_line = [(stn, lax.rem(tm + 2 * i, NT)) for i in range(1, NT // 2)]
    greeted = in_row + in_column + sibling + in_line
    crossed = in_column + in_line

    def v_copy(i):
        qt, h = lax.div(i, 2), lax.rem(i, 2)
        return pltpu.make_async_copy(
            v_ref.at[:, pl.ds(pl.multiple_of(h * 8, 8), 8), pl.ds(pl.multiple_of(qt * 16, 16), 16), :],
            vbuf.at[i],
            v_sem.at[i],
        )

    taps_copy = pltpu.make_async_copy(taps_hbm, taps_ref, c_sem.at[0])
    first = lax.div(y, 2) * 2
    pieces = (first, first + 1, 2 - first, 3 - first)
    v_copy(pieces[0]).start()
    for device in greeted:
        pl.semaphore_signal(barrier, inc=1, device_id=device, device_id_type=MESH)
    for i in pieces[1:]:
        v_copy(i).start()
    taps_copy.start()

    def relayout(j, put):
        d, h = lax.div(j, 2), lax.rem(j, 2)
        yt = lax.rem(y + d, NY)
        at = lax.div(yt, 2) * 2 + h
        odd = lax.rem(yt, 2)
        o = lax.broadcasted_iota(jnp.int32, (LANES, 256), 0)
        c = lax.broadcasted_iota(jnp.int32, (LANES, 256), 1)
        want = ((o >> 3) & 1) * 128 + (o & 7) * 16 + odd * 8 + (o >> 4)
        perm = jnp.where(c == want, 1.0, 0.0).astype(BF16)
        for lane in range(0, N, 512):
            x = vbuf[at, :, :, :, lane : lane + 512].reshape(256, 512)
            turned = jnp.dot(perm, x, preferred_element_type=F32).astype(BF16)
            put(lane, turned.reshape(NZ, ROWS, 512))

    def z_target(j, dz):
        zt = lax.rem(z + dz, NZ)
        yt = lax.rem(y + lax.div(j, 2), NY)
        return zt, (yt * NZ + zt, tm)

    def z_copy(j, dz):
        zt, to = z_target(j, dz)
        return pltpu.make_async_remote_copy(
            src_ref=sb.at[j, zt],
            dst_ref=recv.at[j, z, :, pl.ds(HIST, N)],
            send_sem=zs.at[j],
            recv_sem=zr.at[j],
            device_id=to,
            device_id_type=MESH,
        )

    def own_copy(j):
        return pltpu.make_async_copy(
            sb.at[j, z], recv.at[j, z, :, pl.ds(HIST, N)], zr.at[j]
        )

    def late_copy(j, dz):
        zt, to = z_target(j, dz)
        target = ua if j == FIRST else u_ref
        at = pl.multiple_of(y * 128 + z * 16, 16)
        return pltpu.make_async_remote_copy(
            src_ref=zbuf.at[zt, j - FIRST],
            dst_ref=target.at[:, pl.ds(at, 16), :],
            send_sem=zs.at[j],
            recv_sem=zr.at[j],
            device_id=to,
            device_id_type=MESH,
        )

    def prepare(j):
        def put(lane, tile):
            sb[j, :, :, lane : lane + 512] = tile

        relayout(j, put)

    def send_step(j):
        for dz in ORDER[:-1]:
            z_copy(j, dz).start()

        @pl.when(j < 2)
        def _():
            own_copy(j).start()

        @pl.when(j >= 2)
        def _():
            z_copy(j, 0).start()

    def send_late(j):
        for dz in ORDER:
            late_copy(j, dz).start()

    def wait_step(j):
        whole = recv.at[j, :, :, pl.ds(HIST, N)]
        pltpu.make_async_copy(whole, whole, zr.at[j]).wait()

    def halo_copy(j):
        return pltpu.make_async_remote_copy(
            src_ref=recv.at[j, :, :, pl.ds(N, HIST)],
            dst_ref=recv.at[j, :, :, pl.ds(0, HIST)],
            send_sem=hs.at[j],
            recv_sem=hr.at[j],
            device_id=(stn, lax.rem(tm + 1, NT)),
            device_id_type=MESH,
        )

    def send_halo(j):
        @pl.when(tm < NT - 1)
        def _():
            halo_copy(j).start()

    def wait_halo(j):
        @pl.when(tm > 0)
        def _():
            halo_copy(j).wait_recv()

        @pl.when(tm == 0)
        def _():
            recv[j, :, :, 0:HIST] = jnp.zeros((NZ, ROWS, HIST), BF16)

    def x_copy(j, gp, o):
        to = lax.rem(tm + o, NT)
        return pltpu.make_async_remote_copy(
            src_ref=spec.at[j, gp, pl.ds(to * 8, 8)],
            dst_ref=xg.at[j, tm, gp],
            send_sem=xs.at[j],
            recv_sem=xr.at[j],
            device_id=(stn, to),
            device_id_type=MESH,
        )

    def x_own(j, gp):
        return pltpu.make_async_copy(
            spec.at[j, gp, pl.ds(tm * 8, 8)], xg.at[j, tm, gp], xr.at[j]
        )

    def turn_complex(j, lane):
        o = lax.broadcasted_iota(jnp.int32, (LANES, LANES), 0)
        c = lax.broadcasted_iota(jnp.int32, (LANES, LANES), 1)
        im = (o >> 3) & 1
        sign = (1 - 2 * im).astype(F32)
        turn = jnp.where(c == o + 8 - 16 * im, sign, 0.0).astype(BF16)
        x = recv[j, :, :, lane : lane + 512].reshape(LANES, 512)
        jx[:, lane : lane + 512] = jnp.dot(turn, x, preferred_element_type=F32).astype(BF16)

    def spectra(j, gp):
        lo0 = 1024 * gp
        lo1 = lo0 + 512

        def both(w0, w1, x):
            hi = lax.dot_general(w_hi[w0:w1, :], x, NT_DIMS, preferred_element_type=F32)
            lo = lax.dot_general(w_lo[w0:w1, :], x, NT_DIMS, preferred_element_type=F32)
            return hi + lo

        x = jnp.concatenate(
            [
                recv[j, :, :, lo0 : lo0 + WIN].reshape(LANES, WIN),
                recv[j, :, :, lo1 : lo1 + WIN].reshape(LANES, WIN),
            ],
            axis=0,
        )
        rc[...] = both(0, COS_ROWS, x)
        x = jnp.concatenate([jx[:, lo0 : lo0 + WIN], jx[:, lo1 : lo1 + WIN]], axis=0)
        rs[...] = both(COS_ROWS, COS_ROWS + SIN_ROWS, x)

        def put(k, a):
            tile = jnp.concatenate([a[:, :128], a[:, 128:]], axis=0)
            spec[j, gp, k] = tile.astype(BF16)

        put(0, rc[0:8, :])
        put(32, rc[256:264, :])
        for k in range(1, 32):
            c = rc[8 * k : 8 * k + 8, :]
            s = rs[8 * k : 8 * k + 8, :]
            put(k, c + s)
            put(64 - k, c - s)

    def send_spectra(j, gp):
        def start(o, _):
            x_copy(j, gp, o).start()
            return 0

        lax.fori_loop(1, NT, start, 0)
        x_own(j, gp).start()

    def filterbank(j):
        for lane in range(HIST, HIST + N, 512):
            turn_complex(j, lane)
        spectra(j, 1)
        send_spectra(j, 1)
        wait_halo(j)
        for lane in range(0, HIST, 512):
            turn_complex(j, lane)
        spectra(j, 0)
        send_spectra(j, 0)

    def wait_spectra(j):
        pltpu.make_async_copy(spec.at[j], spec.at[j], xr.at[j]).wait()

    def turn_pair(d, want, put, put_rest):
        wait_spectra(2 * d)
        wait_spectra(2 * d + 1)
        c = lax.broadcasted_iota(jnp.int32, (256, 256), 1)
        perm = jnp.where(c == want, 1.0, 0.0).astype(BF16)

        def channel(k, store):
            a = jnp.concatenate(
                [
                    xg[2 * d, :, :, k].reshape(256, LANES),
                    xg[2 * d + 1, :, :, k].reshape(256, LANES),
                ],
                axis=1,
            )
            t = lax.dot_general(perm, a, NT_DIMS, preferred_element_type=F32)
            lanes = pl.ds(pl.multiple_of((k % 4) * 256, 256), 256)
            store(lanes, t.astype(BF16))

        def early(k, _):
            channel(k, put)
            return 0

        def rest(k, _):
            channel(k, put_rest)
            return 0

        lax.fori_loop(0, 4, early, 0)
        lax.fori_loop(4, 8, rest, 0)

    def rows_of(d):
        return pl.ds(pl.multiple_of(lax.rem(y + NY - d, NY) * 128, 128), 128)

    def u_copy(d):
        return pltpu.make_async_copy(ub.at[d], u_ref.at[:, rows_of(d), :], us.at[d])

    def turn_early(d):
        o = lax.broadcasted_iota(jnp.int32, (256, 256), 0)
        want = ((o >> 3) & 1) * 128 + ((o >> 4) & 7) * 16 + (o >> 7) * 8 + (o & 7)

        def put(lanes, t):
            ua[:, rows_of(d), lanes] = t.reshape(2, 128, 256)

        def put_rest(lanes, t):
            ub[d, :, :, lanes] = t.reshape(2, 128, 256)

        turn_pair(d, want, put, put_rest)
        u_copy(d).start()

    def turn_late():
        o = lax.broadcasted_iota(jnp.int32, (256, 256), 0)
        want = ((o >> 3) & 1) * 128 + (o >> 5) * 16 + ((o >> 4) & 1) * 8 + (o & 7)

        def put(lanes, t):
            zbuf[:, 0, :, :, lanes] = t.reshape(NZ, 2, 16, 256)

        def put_rest(lanes, t):
            zbuf[:, 1, :, :, lanes] = t.reshape(NZ, 2, 16, 256)

        turn_pair(3, want, put, put_rest)

    v_copy(pieces[0]).wait()
    prepare(0)
    pl.semaphore_wait(barrier, len(greeted))
    send_step(0)
    for device in crossed:
        pl.semaphore_signal(round_sem, inc=1, device_id=device, device_id_type=MESH)
    v_copy(pieces[1]).wait()
    prepare(1)
    send_step(1)
    pl.semaphore_wait(round_sem, len(crossed))
    v_copy(pieces[2]).wait()
    v_copy(pieces[3]).wait()

    def prime_late(j, _):
        def put(lane, tile):
            recv[j, :, :, HIST + lane : HIST + lane + 512] = tile

        relayout(j, put)
        send_halo(j)
        return 0

    lax.fori_loop(FIRST, STEPS, prime_late, 0)

    taps_copy.wait()
    half = lax.broadcasted_iota(jnp.int32, (16, 128), 1) < CH
    taps = jnp.concatenate([taps_ref[...], taps_ref[...]], axis=1)
    ppad[...] = jnp.zeros_like(ppad)
    ppad[8:24, :] = jnp.where(half, taps, 0.0)
    ppad[9:25, :] = ppad[9:25, :] + jnp.where(half, 0.0, taps)
    for i in range(WIN // 128):
        tile = ppad[24 - 2 * i : 32 - 2 * i, :]
        t16[:, 128 * i : 128 * i + 128] = jnp.concatenate([tile, tile], axis=0)

    def weights(i, _):
        rows = pl.ds(pl.multiple_of(i * 16, 16), 16)
        sine = (i >= COS_ROWS // 16).astype(jnp.int32)
        r = i * 16 + lax.broadcasted_iota(jnp.int32, (16, 128), 0) - sine * COS_ROWS
        b = lax.broadcasted_iota(jnp.int32, (16, 128), 1)
        turn = ((r >> 3) * b - sine * (CH // 4)) & (CH - 1)
        trig = jnp.cos(turn.astype(F32) * (2 * math.pi / CH)) * (1 / math.sqrt(CH))
        for t in range(WIN // 128):
            lanes = slice(128 * t, 128 * t + 128)
            w = t16[:, lanes] * trig
            hi = w.astype(BF16)
            w_hi[rows, lanes] = hi
            w_lo[rows, lanes] = (w - hi.astype(F32)).astype(BF16)
        return 0

    lax.fori_loop(0, (COS_ROWS + SIN_ROWS) // 16, weights, 0)

    def step(i, _):
        j = jnp.where(i < 2, FIRST + i, i - 2)

        @pl.when(i >= 2)
        def _():
            @pl.when(j + AHEAD < FIRST)
            def _():
                prepare(j + AHEAD)
                send_step(j + AHEAD)

            for late in range(FIRST, STEPS):
                @pl.when(j + AHEAD == late)
                def _(late=late):
                    send_late(late)

            wait_step(j)
            send_halo(j)

        filterbank(j)

        @pl.when(j == LATE_AT)
        def _():
            turn_late()

        @pl.when((j == 3) | (j == 5))
        def _():
            turn_early(lax.div(j - 3, 2))

        return 0

    lax.fori_loop(0, STEPS, step, 0)
    turn_early(2)

    def g_copy(k):
        return pltpu.make_async_copy(gbuf.at[k], g_ref.at[k], gs.at[k])

    wait_step(FIRST)

    def make_gram(k, _):
        lanes = pl.ds(pl.multiple_of(k * 256, 256), 256)
        gram_into(gbuf.at[k], ua[0, :, lanes], ua[1, :, lanes])
        g_copy(k).start()
        return 0

    lax.fori_loop(0, 4, make_gram, 0)

    def finish(j, _):
        @pl.when(j < 2)
        def _():
            part = sb.at[j, pl.ds(0, NZ - 1)]
            pltpu.make_async_copy(part, part, zs.at[j]).wait()

        @pl.when(j >= 2)
        def _():
            part = sb.at[0]
            pltpu.make_async_copy(part, part, zs.at[j]).wait()

        @pl.when(tm < NT - 1)
        def _():
            halo_copy(j).wait_send()

        others = spec.at[j, :, pl.ds(0, 56)]
        pltpu.make_async_copy(others, others, xs.at[j]).wait()
        return 0

    lax.fori_loop(0, STEPS, finish, 0)
    for d in range(3):
        u_copy(d).wait()
    for k in range(4):
        g_copy(k).wait()
    wait_step(STEPS - 1)


LATE_AT = 1


def gram_into(to, re, im, sent=lambda part, rows: None):
    half = 256
    top, bottom = slice(0, half), slice(half, 2 * half)

    def product(left, right):
        g = lax.dot_general(left, right, NT_DIMS, preferred_element_type=F32)
        return (g * (1.0 / 256)).astype(BF16)

    u = jnp.concatenate([re, im], axis=1)
    w = jnp.concatenate([im, -re], axis=1)
    g = product(jnp.concatenate([u[top], w[top]], axis=0), u)
    to[0, top, :] = g[top]
    to[1, top, :] = g[bottom]
    sent(0, pl.ds(0, half))
    sent(1, pl.ds(0, half))
    to[0, bottom, top] = g[top, bottom].T
    to[1, bottom, top] = -(g[bottom, bottom].T)
    g = product(jnp.concatenate([u[bottom], w[bottom]], axis=0), u[bottom])
    to[0, bottom, bottom] = g[top]
    to[1, bottom, bottom] = g[bottom]
    sent(0, pl.ds(half, half))
    sent(1, pl.ds(half, half))


def gram_kernel(u_ref, g_ref, out_ref, held, g_sem, sem):
    copies = [
        pltpu.make_async_copy(g_ref.at[k], out_ref.at[0, k], g_sem.at[k]) for k in range(4)
    ]
    for c in copies:
        c.start()
    for k in range(4):
        lanes = slice(256 * k, 256 * k + 256)

        def sent(part, rows, k=k):
            c = pltpu.make_async_copy(
                held.at[k, part, rows],
                out_ref.at[0, k + 4, part, rows],
                sem.at[len(copies) - 4],
            )
            c.start()
            copies.append(c)

        gram_into(held.at[k], u_ref[0, :, lanes], u_ref[1, :, lanes], sent)
    for c in copies:
        c.wait()


def body(voltages, fir_taps):
    dma = pltpu.SemaphoreType.DMA
    any_space = pl.BlockSpec(memory_space=pl.ANY)
    u, g = pl.pallas_call(
        comm_kernel,
        out_shape=[
            jax.ShapeDtypeStruct((2, 512, 4 * 256), BF16),
            jax.ShapeDtypeStruct((4, 2, 512, 512), BF16),
        ],
        in_specs=[pl.BlockSpec(memory_space=pltpu.HBM)] * 2,
        out_specs=[any_space, any_space],
        scratch_shapes=[
            pltpu.VMEM((4, 2, 8, 16, N), BF16),
            pltpu.VMEM((16, CH), F32),
            pltpu.VMEM((FIRST, NZ, ROWS, N), BF16),
            pltpu.VMEM((STEPS, NZ, ROWS, HIST + N), BF16),
            pltpu.VMEM((LANES, HIST + N), BF16),
            pltpu.VMEM((STEPS, 2, CH, 16, 128), BF16),
            pltpu.VMEM((STEPS, NT, 2, 8, 16, 128), BF16),
            pltpu.VMEM((2, 512, 4 * 256), BF16),
            pltpu.VMEM((3, 2, 128, 4 * 256), BF16),
            pltpu.VMEM((NZ, 2, 2, 16, 4 * 256), BF16),
            pltpu.VMEM((4, 2, 512, 512), BF16),
            pltpu.VMEM((COS_ROWS + SIN_ROWS, WIN), BF16),
            pltpu.VMEM((COS_ROWS + SIN_ROWS, WIN), BF16),
            pltpu.VMEM((32, 128), F32),
            pltpu.VMEM((16, WIN), F32),
            pltpu.VMEM((COS_ROWS, 256), F32),
            pltpu.VMEM((SIN_ROWS, 256), F32),
            pltpu.SemaphoreType.REGULAR,
            dma((4,)),
            dma((1,)),
        ]
        + [dma((STEPS,))] * 6
        + [dma((3,)), dma((4,))],
        compiler_params=pltpu.CompilerParams(
            collective_id=0, has_side_effects=True, vmem_limit_bytes=44 * 2**20
        ),
        name="exchange",
    )(voltages, fir_taps)
    return pl.pallas_call(
        gram_kernel,
        out_shape=jax.ShapeDtypeStruct((1, 8, 2, 512, 512), BF16),
        in_specs=[pl.BlockSpec(memory_space=pltpu.VMEM), any_space],
        out_specs=any_space,
        scratch_shapes=[pltpu.VMEM((4, 2, 512, 512), BF16), dma((4,)), dma((16,))],
        compiler_params=pltpu.CompilerParams(vmem_limit_bytes=24 * 2**20),
        name="gram",
    )(u, g)


def solution(mesh):
    return jax.shard_map(
        body,
        mesh=mesh,
        in_specs=(P(None, "stn", None, "tm"), P()),
        out_specs=P("stn", "tm", None, None, None),
        check_vma=False,
    )
```
